32 devices in a mesh: dp: 2 (over y), tile: 16 (over z, x, core).
Axes of the slice: x: 2, y: 2, z: 4, core: 2. Of those that a mesh axis runs over, the one named last changes fastest.
Arguments:
- videos: bfloat16 [2, 16, 32, 64, 512], P('dp', 'tile'), may hold values from -6 to 6
- spatial_filter: bfloat16 [9, 512, 512], P(None, 'dp'), may hold values from -0.09375 to 0.09375
- temporal_filter: bfloat16 [3, 512, 512], P(None, 'dp'), may hold values from -0.15625 to 0.15625
- spatial_bias: float32 [512], replicated, may hold values from -3 to 3
- temporal_bias: float32 [512], replicated, may hold values from -3 to 3
Outputs:
- output: bfloat16 [2, 16, 32, 64, 512], P('dp', 'tile')
The draws below stay inside these ranges and needn't reach their ends.
All inputs are finite; a program needn't handle non-finite values.
Results may differ from the reference program's by a relative error of at most 0.0044.
Values may be sent and summed in bfloat16 or wider, within the bound.
No kernel may reach another device: no remote copies, remote signals or barrier semaphores. Data moves between devices by JAX's collectives and lax.ppermute only.
A program may use at most 128 MiB of HBM per device.

```python
import jax
import jax.numpy as jnp
from jax import lax

C = 512
HH = 32
WW = 64
SAMPLES = 2
FRAMES = 16


def block_levels(own_key, shape, split, smallest, largest):
    factor_of, own = 1.0, jax.random.fold_in(own_key, 6)
    for axis_at, blocks in split:
        steps = jnp.exp(jax.random.uniform(jax.random.fold_in(own, axis_at), (blocks,), jnp.float32, smallest / len(split), largest / len(split)))
        factor_of = factor_of * jnp.repeat(steps, shape[axis_at] // blocks).reshape([-1 if axis == axis_at else 1 for axis in range(len(shape))])
    return factor_of


def bell_draw(key, extent, spread, most, pieces=(), dtype=jnp.bfloat16):
    gain = block_levels(key, extent, pieces, -0.22, 0.18) if pieces else 1.0
    entries = jax.random.normal(key, extent, jnp.float32) * spread * gain
    return jnp.minimum(jnp.maximum(entries, -most), most).astype(dtype)


def setup_inputs(seed: int = 0) -> dict:
    key_list = jax.random.split(jax.random.key(seed), 6)
    return {
        "videos": bell_draw(key_list[0], (SAMPLES, FRAMES, HH, WW, C), 1.0, 6.0, ((0, 2), (1, 16))),
        "spatial_filter": bell_draw(key_list[1], (9, C, C), (9 * C) ** -0.5, 0.09375, ((1, 2),)),
        "temporal_filter": bell_draw(key_list[2], (3, C, C), (3 * C) ** -0.5, 0.15625, ((1, 2),)),
        "spatial_bias": bell_draw(key_list[3], (C,), 0.5, 3.0, (), jnp.float32),
        "temporal_bias": bell_draw(key_list[4], (C,), 0.5, 3.0, (), jnp.float32),
    }


def reference(videos, spatial_filter, temporal_filter, spatial_bias, temporal_bias):
    def one_sample(video):
        frames, height, breadth, channels = video.shape
        padded = jnp.pad(video, ((0, 0), (1, 1), (1, 1), (0, 0)))
        summed = jnp.zeros((frames * height * breadth, channels), jnp.float32)
        for row_off in range(3):
            for col_off in range(3):
                window = padded[:, row_off:row_off + height, col_off:col_off + breadth, :].reshape(-1, channels)
                summed = summed + jnp.dot(window, spatial_filter[3 * row_off + col_off], preferred_element_type=jnp.float32)
        hidden = jax.nn.silu(summed + spatial_bias).astype(jnp.bfloat16).reshape(frames, height, breadth, channels)
        framed = jnp.pad(hidden, ((1, 1), (0, 0), (0, 0), (0, 0)))
        result = jnp.zeros((frames * height * breadth, channels), jnp.float32)
        for lag in range(3):
            window = framed[lag:lag + frames].reshape(-1, channels)
            result = result + jnp.dot(window, temporal_filter[lag], preferred_element_type=jnp.float32)
        return (result + temporal_bias).astype(jnp.bfloat16).reshape(video.shape)

    return lax.map(one_sample, videos)
```

```python
import functools

import jax
import jax.numpy as jnp
from jax import lax
from jax.experimental import pallas as pl
from jax.experimental.pallas import tpu as pltpu
from jax.sharding import PartitionSpec as P

TAPS = (1, 4, 7, 0, 3, 6, 2, 5, 8)
VMEM = 60 * 2**20


def dot(a, b):
    return jnp.dot(a, b, preferred_element_type=jnp.float32)


def silu(v):
    return v / (1 + jnp.exp(-v))


def rows_conv(padded, weights, first, rows, breadth, columns, ready=None):
    count = rows * breadth
    place = lax.rem(lax.broadcasted_iota(jnp.int32, (count, 1), 0), breadth)
    depth = padded.shape[2]
    lines = jnp.concatenate(
        [padded[pl.ds(first + dy, rows)].reshape(count, depth) for dy in range(3)], axis=1
    )

    def side(dx):
        if ready is not None:
            ready(dx)
        matrix = jnp.concatenate([weights[3 * dy + dx, :, columns] for dy in range(3)], axis=0)
        return dot(lines, matrix)

    total = side(1)
    total += jnp.where(place == 0, 0.0, pltpu.roll(side(0), 1, 0))
    total += jnp.where(place == breadth - 1, 0.0, pltpu.roll(side(2), count - 1, 0))
    return total


def halves(width):
    cut = width // 2
    return [slice(0, cut), slice(cut, width)]


def conv_kernel(rows, pieces, has_base, activate, at_ref, *refs):
    video = refs[0]
    parts = refs[1 : 1 + pieces]
    rest = refs[1 + pieces :]
    base = rest[0] if has_base else None
    bias, out, padded, weights, video_sem, part_sem = rest[1 if has_base else 0 :]
    height, breadth = video.shape[0], video.shape[1]
    depth = padded.shape[2]
    steps = height // rows
    i = pl.program_id(0)

    def video_copy(j):
        channels = pl.ds(pl.multiple_of(at_ref[0], 128), depth)
        return pltpu.make_async_copy(
            video.at[pl.ds(j * rows, rows), :, channels], padded.at[pl.ds(j * rows + 1, rows)], video_sem.at[j]
        )

    def part_copy(p, tap):
        deep = parts[p].shape[1]
        begin = 0 if pieces == 1 else pl.multiple_of(at_ref[1 + p], 64)
        return pltpu.make_async_copy(
            parts[p].at[tap], weights.at[tap, pl.ds(begin, deep)], part_sem.at[p, tap]
        )

    @pl.when(i == 0)
    def _():
        video_copy(0).start()
        for tap in TAPS[:3]:
            for p in range(pieces):
                part_copy(p, tap).start()
        if steps > 1:
            video_copy(1).start()
        for tap in TAPS[3:]:
            for p in range(pieces):
                part_copy(p, tap).start()
        for j in range(2, steps):
            video_copy(j).start()
        padded[0] = jnp.zeros(padded.shape[1:], padded.dtype)
        padded[height + 1] = jnp.zeros(padded.shape[1:], padded.dtype)
        video_copy(0).wait()
        for tap in TAPS:
            for p in range(pieces):
                part_copy(p, tap).wait()

    @pl.when(i + 1 < steps)
    def _():
        video_copy(i + 1).wait()

    for columns in halves(out.shape[2]):
        total = rows_conv(padded, weights, i * rows, rows, breadth, columns)
        if has_base:
            total += base[:, :, columns].reshape(total.shape)
        if activate:
            total = silu(total + bias[:, columns])
        out[:, :, columns] = total.astype(out.dtype).reshape(rows, breadth, -1)


def conv_call(video, parts, at, base, bias, depth, rows, activate):
    height, breadth, channels = video.shape
    width = parts[0].shape[2]
    steps = height // rows
    has_base = base is not None
    row_spec = pl.BlockSpec((rows, breadth, width), lambda i, at: (i, 0, 0))
    any_spec = pl.BlockSpec(memory_space=pl.ANY)
    operands = [video, *parts] + ([base] if has_base else []) + [bias]
    return pl.pallas_call(
        functools.partial(conv_kernel, rows, len(parts), has_base, activate),
        grid_spec=pltpu.PrefetchScalarGridSpec(
            num_scalar_prefetch=1,
            grid=(steps,),
            in_specs=[any_spec] * (1 + len(parts))
            + ([row_spec] if has_base else [])
            + [pl.BlockSpec((1, width), lambda i, at: (0, 0))],
            out_specs=row_spec,
            scratch_shapes=[
                pltpu.VMEM((height + 2, breadth, depth), video.dtype),
                pltpu.VMEM((9, depth, width), video.dtype),
                pltpu.SemaphoreType.DMA((steps,)),
                pltpu.SemaphoreType.DMA((len(parts), 9)),
            ],
        ),
        out_shape=jax.ShapeDtypeStruct((height, breadth, width), jnp.bfloat16 if activate else jnp.float32),
        cost_estimate=pl.CostEstimate(
            flops=2 * height * breadth * 9 * depth * width, bytes_accessed=12 * 2**20, transcendentals=0
        ),
        compiler_params=pltpu.CompilerParams(vmem_limit_bytes=VMEM),
    )(at, *operands)


def far_kernel(rows, top, begin, pieces, at_ref, *refs):
    blocks = refs[:top]
    parts = refs[top : top + pieces]
    bias, out, padded, weights, video_sem, part_sem = refs[top + pieces :]
    breadth = out.shape[1]
    steps = pl.num_programs(0)
    i = pl.program_id(0)
    need = padded.shape[0]

    def video_copies():
        copies, at = [], 0
        low = begin - 1
        for p, block in enumerate(blocks):
            size = block.shape[0]
            start, end = max(low, at), min(low + need, at + size)
            if end > start:
                copies.append(
                    pltpu.make_async_copy(
                        block.at[pl.ds(start - at, end - start)],
                        padded.at[pl.ds(start - low, end - start)],
                        video_sem.at[p],
                    )
                )
            at += size
        return copies

    def part_copy(p, tap):
        deep = parts[p].shape[1]
        first = 0 if pieces == 1 else pl.multiple_of(at_ref[1 + p], 64)
        return pltpu.make_async_copy(
            parts[p].at[tap], weights.at[tap, pl.ds(first, deep)], part_sem.at[p, tap]
        )

    @pl.when(i == 0)
    def _():
        for copy in video_copies():
            copy.start()
        for tap in TAPS:
            for p in range(pieces):
                part_copy(p, tap).start()
        if begin == 0:
            padded[0] = jnp.zeros(padded.shape[1:], padded.dtype)
        for copy in video_copies():
            copy.wait()
        for tap in TAPS:
            for p in range(pieces):
                part_copy(p, tap).wait()

    for columns in halves(out.shape[2]):
        total = rows_conv(padded, weights, i * rows, rows, breadth, columns)
        total = silu(total + bias[:, columns])
        out[:, :, columns] = total.astype(out.dtype).reshape(rows, breadth, -1)


def far_call(blocks, parts, at, bias, begin, count, rows):
    breadth, channels = blocks[0].shape[1:]
    width = parts[0].shape[2]
    any_spec = pl.BlockSpec(memory_space=pl.ANY)
    return pl.pallas_call(
        functools.partial(far_kernel, rows, len(blocks), begin, len(parts)),
        grid_spec=pltpu.PrefetchScalarGridSpec(
            num_scalar_prefetch=1,
            grid=(count // rows,),
            in_specs=[any_spec] * (len(blocks) + len(parts)) + [pl.BlockSpec((1, width), lambda i, at: (0, 0))],
            out_specs=pl.BlockSpec((rows, breadth, width), lambda i, at: (i, 0, 0)),
            scratch_shapes=[
                pltpu.VMEM((count + 2, breadth, channels), blocks[0].dtype),
                pltpu.VMEM((9, channels, width), blocks[0].dtype),
                pltpu.SemaphoreType.DMA((len(blocks),)),
                pltpu.SemaphoreType.DMA((len(parts), 9)),
            ],
        ),
        out_shape=jax.ShapeDtypeStruct((count, breadth, width), jnp.bfloat16),
        cost_estimate=pl.CostEstimate(
            flops=2 * count * breadth * 9 * channels * width, bytes_accessed=8 * 2**20, transcendentals=0
        ),
        compiler_params=pltpu.CompilerParams(vmem_limit_bytes=VMEM),
    )(at, *blocks, *parts, bias)


def mix_kernel(pieces, aliased, at_ref, own, mate, far, *refs):
    parts = refs[:pieces]
    bias, out, weights, part_sem = refs[pieces + aliased :]
    rows, breadth, width = out.shape
    depth = weights.shape[1]
    i = pl.program_id(0)

    def part_copy(p):
        deep = parts[p].shape[1]
        first = 0 if pieces == 1 else pl.multiple_of(at_ref[3 + p], 64)
        return pltpu.make_async_copy(parts[p], weights.at[:, pl.ds(first, deep)], part_sem.at[p])

    @pl.when(i == 0)
    def _():
        for p in range(pieces):
            part_copy(p).start()
        for p in range(pieces):
            part_copy(p).wait()

    count = rows * breadth
    lines = [ref[...].reshape(count, depth) for ref in (own, mate, far)]
    lines[2] = jnp.where(at_ref[2] > 0, lines[2], jnp.zeros_like(lines[2]))
    for columns in halves(width):
        total = dot(lines[0], weights[1, :, columns])
        total += dot(lines[1], weights[at_ref[0], :, columns])
        total += dot(lines[2], weights[at_ref[1], :, columns])
        total += bias[:, columns]
        out[:, :, columns] = total.astype(out.dtype).reshape(rows, breadth, -1)


def mix_call(own, mate, far, parts, at, bias, before, begin, rows):
    height, breadth, depth = own.shape
    width = parts[0].shape[2]
    count = far.shape[0]
    any_spec = pl.BlockSpec(memory_space=pl.ANY)
    there = pl.BlockSpec((rows, breadth, depth), lambda i, at: (i + begin // rows, 0, 0))
    aliased = 0 if before is None else 1
    return pl.pallas_call(
        functools.partial(mix_kernel, len(parts), aliased),
        grid_spec=pltpu.PrefetchScalarGridSpec(
            num_scalar_prefetch=1,
            grid=(count // rows,),
            in_specs=[there, there, pl.BlockSpec((rows, breadth, depth), lambda i, at: (i, 0, 0))]
            + [any_spec] * (len(parts) + aliased)
            + [pl.BlockSpec((1, width), lambda i, at: (0, 0))],
            out_specs=pl.BlockSpec((rows, breadth, width), lambda i, at: (i + begin // rows, 0, 0)),
            scratch_shapes=[
                pltpu.VMEM((3, depth, width), own.dtype),
                pltpu.SemaphoreType.DMA((len(parts),)),
            ],
        ),
        out_shape=jax.ShapeDtypeStruct((height, breadth, width), jnp.bfloat16),
        input_output_aliases={4 + len(parts): 0} if aliased else {},
        cost_estimate=pl.CostEstimate(
            flops=2 * count * breadth * 3 * depth * width, bytes_accessed=6 * 2**20, transcendentals=0
        ),
        compiler_params=pltpu.CompilerParams(vmem_limit_bytes=VMEM),
    )(at, own, mate, far, *parts, *([before] if aliased else []), bias)


def near_device(videos, spatial_filter, temporal_filter, spatial_bias, temporal_bias):
    height, breadth, channels = videos.shape[2:]
    video = videos.reshape(height, breadth, channels)
    spatial_bias = spatial_bias.reshape(1, -1)
    temporal_bias = temporal_bias.reshape(1, -1)
    tiles = lax.axis_size("tile")
    group, tile = lax.axis_index("dp"), lax.axis_index("tile")
    core = lax.rem(tile, 2)
    depth = spatial_filter.shape[1]
    part = depth // 2
    swap = [(0, 1), (1, 0)]
    mates = [(i, i ^ 1) for i in range(tiles)]
    across = [pair for i in range(1, tiles - 1, 2) for pair in ((i, i + 1), (i + 1, i))]

    first, second = height // 2, 3 * height // 4
    far_a = lax.ppermute(video[: first + 1], "tile", across)
    mine = lax.dynamic_slice_in_dim(spatial_filter, core * part, part, axis=1)
    spatial_y = lax.ppermute(mine, "dp", swap)
    mine = lax.dynamic_slice_in_dim(temporal_filter, core * part, part, axis=1)
    temporal_y = lax.ppermute(mine, "dp", swap)
    far_b = lax.ppermute(video[first + 1 : second + 1], "tile", across)
    spatial_m = lax.ppermute(spatial_y, "tile", mates)
    temporal_m = lax.ppermute(temporal_y, "tile", mates)

    here, there = group * depth, (1 - group) * depth
    local = conv_call(
        video, [spatial_filter], jnp.stack([here]), None, spatial_bias, depth, 8, False
    )
    at = jnp.stack([there, core * part, (1 - core) * part])
    hidden = conv_call(video, [spatial_y, spatial_m], at, local, spatial_bias, depth, 8, True)
    mate = lax.ppermute(hidden, "tile", mates)
    far_c = lax.ppermute(hidden[second:], "tile", across)
    places = [here, there + core * part, there + (1 - core) * part]
    at = jnp.stack([here, *places])
    parts = [spatial_filter, spatial_y, spatial_m]
    hidden_a = far_call([far_a], parts, at, spatial_bias, 0, first, 8)
    hidden_b = far_call([far_a, far_b], parts, at, spatial_bias, first, second - first, 8)
    present = jnp.where(core == 0, tile > 0, tile < tiles - 1).astype(jnp.int32)
    at = jnp.stack([2 - 2 * core, 2 * core, present, *places])
    parts = [temporal_filter, temporal_y, temporal_m]
    out = mix_call(hidden, mate, hidden_a, parts, at, temporal_bias, None, 0, 8)
    out = mix_call(hidden, mate, hidden_b, parts, at, temporal_bias, out, first, 8)
    out = mix_call(hidden, mate, far_c, parts, at, temporal_bias, out, second, 8)
    return out.reshape(videos.shape)


def padded_2(block, sides, width):
    for axis, dim in sides:
        count = lax.axis_size(axis)
        forward = [(i, i + 1) for i in range(count - 1)]
        backward = [(target, source) for source, target in forward]
        low = lax.ppermute(
            lax.slice_in_dim(block, block.shape[dim] - width, None, axis=dim), axis, forward
        )
        high = lax.ppermute(lax.slice_in_dim(block, 0, width, axis=dim), axis, backward)
        block = jnp.concatenate([low, block, high], axis=dim)
    return block


def spatial_term(padded, weight_piece):
    width = weight_piece.shape[1]
    height = padded.shape[2] - 2
    breadth = padded.shape[3] - 2
    columns = jnp.concatenate(
        [
            padded[:, :, row_off : row_off + height, col_off : col_off + breadth, :]
            for row_off in range(3)
            for col_off in range(3)
        ],
        axis=4,
    )
    matrix = weight_piece.reshape(9 * width, weight_piece.shape[2])
    return jnp.dot(columns.reshape(-1, 9 * width), matrix, preferred_element_type=jnp.float32)


def temporal_term(framed, weight_piece):
    width = weight_piece.shape[1]
    frames = framed.shape[1] - 2
    columns = jnp.concatenate([framed[:, lag : lag + frames] for lag in range(3)], axis=4)
    matrix = weight_piece.reshape(3 * width, weight_piece.shape[2])
    return jnp.dot(columns.reshape(-1, 3 * width), matrix, preferred_element_type=jnp.float32)


def any_device(videos, spatial_filter, temporal_filter, spatial_bias, temporal_bias):
    samples, frames, height, breadth, channels = videos.shape
    padded = jnp.pad(videos, ((0, 0), (0, 0), (1, 1), (1, 1), (0, 0)))
    summed = spatial_term(padded, lax.all_gather(spatial_filter, "dp", axis=1, tiled=True))
    activated = jax.nn.silu(summed + spatial_bias).astype(jnp.bfloat16)
    hidden = activated.reshape(samples, frames, height, breadth, channels)
    framed = padded_2(hidden, (("tile", 1),), 1)
    result = temporal_term(framed, lax.all_gather(temporal_filter, "dp", axis=1, tiled=True))
    return (result + temporal_bias).astype(jnp.bfloat16).reshape(videos.shape)


def per_device(videos, *rest):
    near = (
        videos.shape[0] == 1
        and videos.shape[1] == 1
        and videos.shape[2] % 32 == 0
        and lax.axis_size("dp") == 2
        and lax.axis_size("tile") % 2 == 0
    )
    return (near_device if near else any_device)(videos, *rest)


def solution(mesh):
    return jax.shard_map(
        per_device,
        mesh=mesh,
        in_specs=(
            P("dp", "tile", None, None, None),
            P(None, "dp", None),
            P(None, "dp", None),
            P(),
            P(),
        ),
        out_specs=P("dp", "tile", None, None, None),
        check_vma=False,
    )
```

```python
import functools

import jax
import jax.numpy as jnp
from jax import lax
from jax.experimental import pallas as pl
from jax.experimental.pallas import tpu as pltpu
from jax.sharding import PartitionSpec as P

ANY = pl.BlockSpec(memory_space=pltpu.HBM)


def dot(a, b):
    return jnp.dot(a, b, preferred_element_type=jnp.float32)


def silu(v):
    return v / (1 + jnp.exp(-v))


def halves(width):
    cut = width // 2
    return [slice(0, cut), slice(cut, width)]


def seat():
    tile = lax.axis_index("tile")
    return lax.axis_index("dp"), lax.rem(tile // 4, 2), lax.rem(tile, 2)


def piece_rows(depth):
    return 3 * depth // 16, depth // 8


def piece_starts(depth):
    _, pair, core = seat()
    small, large = piece_rows(depth)
    near = [(pair, core), (1 - pair, core), (pair, 1 - core), (1 - pair, 1 - core)]
    return [(2 * p + c) * small for p, c in near] + [4 * small + c * large for c in (core, 1 - core)]


def aligned(start):
    return pl.multiple_of(start, 16)


def rows_conv(padded, weights, first, rows, breadth, columns):
    count = rows * breadth
    place = lax.rem(lax.broadcasted_iota(jnp.int32, (count, 1), 0), breadth)
    depth = padded.shape[2]
    lines = jnp.concatenate(
        [padded[pl.ds(first + dy, rows)].reshape(count, depth) for dy in range(3)], axis=1
    )

    def side(dx):
        matrix = jnp.concatenate([weights[3 * dy + dx, :, columns] for dy in range(3)], axis=0)
        return dot(lines, matrix)

    total = side(1)
    total += jnp.where(place == 0, 0.0, pltpu.roll(side(0), 1, 0))
    total += jnp.where(place == breadth - 1, 0.0, pltpu.roll(side(2), count - 1, 0))
    return total


def base_kernel(rows, video, part, out, padded, weights, video_sem, part_sem):
    height, breadth = video.shape[:2]
    depth = part.shape[1]
    steps = height // rows
    i = pl.program_id(0)
    group = lax.axis_index("dp")

    def video_copy(j):
        channels = pl.ds(pl.multiple_of(group * depth, 128), depth)
        return pltpu.make_async_copy(
            video.at[pl.ds(j * rows, rows), :, channels],
            padded.at[pl.ds(j * rows + 1, rows)],
            video_sem.at[j],
        )

    part_copy = pltpu.make_async_copy(part, weights, part_sem)

    @pl.when(i == 0)
    def _():
        video_copy(0).start()
        part_copy.start()
        for j in range(1, steps):
            video_copy(j).start()
        padded[0] = jnp.zeros(padded.shape[1:], padded.dtype)
        padded[height + 1] = jnp.zeros(padded.shape[1:], padded.dtype)
        video_copy(0).wait()
        part_copy.wait()

    @pl.when(i + 1 < steps)
    def _():
        video_copy(i + 1).wait()

    for columns in halves(out.shape[2]):
        total = rows_conv(padded, weights, i * rows, rows, breadth, columns)
        out[:, :, columns] = total.reshape(rows, breadth, -1)


def base_call(video, part, rows, cost):
    height, breadth, _ = video.shape
    depth, width = part.shape[1:]
    steps = height // rows
    return pl.pallas_call(
        functools.partial(base_kernel, rows),
        grid=(steps,),
        in_specs=[ANY, ANY],
        out_specs=pl.BlockSpec((rows, breadth, width), lambda i: (i, 0, 0)),
        scratch_shapes=[
            pltpu.VMEM((height + 2, breadth, depth), video.dtype),
            pltpu.VMEM((9, depth, width), video.dtype),
            pltpu.SemaphoreType.DMA((steps,)),
            pltpu.SemaphoreType.DMA,
        ],
        out_shape=jax.ShapeDtypeStruct((height, breadth, width), jnp.float32),
        cost_estimate=cost,
        compiler_params=pltpu.CompilerParams(vmem_limit_bytes=24 * 2**20),
    )(video, part)


def own_kernel(rows, pieces, video, base, bias, *refs):
    parts = refs[:pieces]
    height, breadth = video.shape[:2]
    steps = height // rows
    outs = refs[pieces : pieces + steps]
    padded, weights, hidden, video_sem, part_sem, out_sem = refs[pieces + steps :]
    depth = weights.shape[1]
    i = pl.program_id(0)
    group = lax.axis_index("dp")
    starts = piece_starts(depth)

    def video_copy(j):
        channels = pl.ds(pl.multiple_of((1 - group) * depth, 128), depth)
        return pltpu.make_async_copy(
            video.at[pl.ds(j * rows, rows), :, channels],
            padded.at[pl.ds(j * rows + 1, rows)],
            video_sem.at[j],
        )

    def part_copy(p):
        there = weights.at[:, pl.ds(aligned(starts[p]), parts[p].shape[1])]
        return pltpu.make_async_copy(parts[p], there, part_sem.at[p])

    def out_copy(j):
        return pltpu.make_async_copy(hidden.at[j], outs[j], out_sem.at[j])

    @pl.when(i == 0)
    def _():
        video_copy(0).start()
        for p in range(pieces):
            part_copy(p).start()
        for j in range(1, steps):
            video_copy(j).start()
        padded[0] = jnp.zeros(padded.shape[1:], padded.dtype)
        padded[height + 1] = jnp.zeros(padded.shape[1:], padded.dtype)
        video_copy(0).wait()
        for p in range(pieces):
            part_copy(p).wait()

    @pl.when(i + 1 < steps)
    def _():
        video_copy(i + 1).wait()

    for columns in halves(weights.shape[2]):
        total = rows_conv(padded, weights, i * rows, rows, breadth, columns)
        total = silu(total + base[:, :, columns].reshape(total.shape) + bias[:, columns])
        hidden[i, :, :, columns] = total.astype(hidden.dtype).reshape(rows, breadth, -1)

    for j in range(steps):

        @pl.when(i == j)
        def _():
            out_copy(j).start()

    @pl.when(i == steps - 1)
    def _():
        for j in range(steps):
            out_copy(j).wait()


def own_call(video, base, bias, parts, depth, rows, cost):
    height, breadth, _ = video.shape
    width = base.shape[2]
    steps = height // rows
    return pl.pallas_call(
        functools.partial(own_kernel, rows, len(parts)),
        grid=(steps,),
        in_specs=[
            ANY,
            pl.BlockSpec((rows, breadth, width), lambda i: (i, 0, 0)),
            pl.BlockSpec((1, width), lambda i: (0, 0)),
        ]
        + [ANY] * len(parts),
        out_specs=[ANY] * steps,
        scratch_shapes=[
            pltpu.VMEM((height + 2, breadth, depth), video.dtype),
            pltpu.VMEM((9, depth, width), video.dtype),
            pltpu.VMEM((steps, rows, breadth, width), video.dtype),
            pltpu.SemaphoreType.DMA((steps,)),
            pltpu.SemaphoreType.DMA((len(parts),)),
            pltpu.SemaphoreType.DMA((steps,)),
        ],
        out_shape=[jax.ShapeDtypeStruct((rows, breadth, width), video.dtype)] * steps,
        cost_estimate=cost,
        compiler_params=pltpu.CompilerParams(vmem_limit_bytes=24 * 2**20),
    )(video, base, bias, *parts)


def mix_kernel(rows, begin, blocks, given, pieces, aliased, tiles, *refs):
    refs = list(refs)

    def take(count):
        taken = refs[:count]
        del refs[:count]
        return taken

    steps = pl.num_programs(0)
    owns, mates = take(blocks), take(blocks)
    fars = take(blocks if given else 1)
    temporal_parts = take(1 + pieces[1])
    spatial_parts = [] if given else take(1 + pieces[0])
    spatial_bias, temporal_bias = take(2)
    take(aliased)
    (out,) = take(1)
    own, mate, far, temporal, spatial, row_sem, mate_sem, far_sem, temporal_sem, spatial_sem = refs
    breadth, width = out.shape[1:]
    depth = temporal.shape[1]
    group, _, core = seat()
    tile = lax.axis_index("tile")
    present = jnp.where(core == 0, tile > 0, tile < tiles - 1)
    i = pl.program_id(0)

    def part_copies(parts, weights, sem):
        held = parts[0].shape[1]
        there = (1 - group) * held
        if len(parts) == 3:
            starts = [group * held, there + core * (held // 2), there + (1 - core) * (held // 2)]
        else:
            starts = [group * held] + [there + start for start in piece_starts(held)]
        return [
            pltpu.make_async_copy(
                part, weights.at[:, pl.ds(aligned(start), part.shape[1])], sem.at[p]
            )
            for p, (part, start) in enumerate(zip(parts, starts, strict=True))
        ]

    def block_copies(sources, target, sem):
        return [
            pltpu.make_async_copy(source, target.at[pl.ds(p * source.shape[0], source.shape[0])], sem.at[p])
            for p, source in enumerate(sources)
        ]

    def far_copies():
        if given:
            return block_copies(fars, far, far_sem)
        low = begin - 1
        start, end = max(low, 0), min(low + far.shape[0], fars[0].shape[0])
        return [
            pltpu.make_async_copy(
                fars[0].at[pl.ds(start, end - start)], far.at[pl.ds(start - low, end - start)], far_sem.at[0]
            )
        ]

    first = part_copies(temporal_parts, temporal, temporal_sem)
    first += block_copies(owns, own, row_sem) + block_copies(mates, mate, mate_sem)
    second = far_copies() + ([] if given else part_copies(spatial_parts, spatial, spatial_sem))

    @pl.when(i == 0)
    def _():
        for copy in first + second:
            copy.start()
        if not given and begin == 0:
            far[0] = jnp.zeros(far.shape[1:], far.dtype)
        for copy in first:
            copy.wait()

    count = rows * breadth
    here = pl.ds(i * rows, rows)
    own_lines = own[here].reshape(count, depth)
    mate_lines = mate[here].reshape(count, depth)
    mate_tap, far_tap = 2 - 2 * core, 2 * core
    totals = [
        dot(own_lines, temporal[1, :, columns]) + dot(mate_lines, temporal[mate_tap, :, columns])
        for columns in halves(width)
    ]

    @pl.when(i == 0)
    def _():
        for copy in second:
            copy.wait()

    if given:
        far_lines = far[here].reshape(count, depth)
    else:
        far_lines = jnp.concatenate(
            [
                silu(rows_conv(far, spatial, i * rows, rows, breadth, columns) + spatial_bias[:, columns]).astype(
                    far.dtype
                )
                for columns in halves(depth)
            ],
            axis=1,
        )
    far_lines = jnp.where(present, far_lines, jnp.zeros_like(far_lines))
    for total, columns in zip(totals, halves(width), strict=True):
        total += dot(far_lines, temporal[far_tap, :, columns]) + temporal_bias[:, columns]
        out[:, :, columns] = total.astype(out.dtype).reshape(rows, breadth, -1)


def mix_call(shape, owns, mates, fars, given, temporal_parts, spatial_parts, biases, before, begin, rows, tiles, cost):
    height, breadth, width = shape
    dtype = owns[0].dtype
    count = sum(own.shape[0] for own in owns)
    depth = owns[0].shape[2]
    aliased = 0 if before is None else 1
    operands = [*owns, *mates, *fars, *temporal_parts, *spatial_parts]
    whole = pl.BlockSpec((1, width), lambda i: (0, 0))
    pieces = (len(spatial_parts) - 1, len(temporal_parts) - 1)
    return pl.pallas_call(
        functools.partial(mix_kernel, rows, begin, len(owns), given, pieces, aliased, tiles),
        grid=(count // rows,),
        in_specs=[ANY] * len(operands) + [whole, whole] + [ANY] * aliased,
        out_specs=pl.BlockSpec((rows, breadth, width), lambda i: (i + begin // rows, 0, 0)),
        scratch_shapes=[
            pltpu.VMEM((count, breadth, depth), dtype),
            pltpu.VMEM((count, breadth, depth), dtype),
            pltpu.VMEM((count if given else count + 2, breadth, depth), dtype),
            pltpu.VMEM((3, depth, width), dtype),
            pltpu.VMEM((8, 128) if given else (9, depth, depth), dtype),
            pltpu.SemaphoreType.DMA((len(owns),)),
            pltpu.SemaphoreType.DMA((len(owns),)),
            pltpu.SemaphoreType.DMA((len(fars),)),
            pltpu.SemaphoreType.DMA((len(temporal_parts),)),
            pltpu.SemaphoreType.DMA((max(len(spatial_parts), 1),)),
        ],
        out_shape=jax.ShapeDtypeStruct(shape, dtype),
        input_output_aliases={len(operands) + 2: 0} if aliased else {},
        cost_estimate=cost,
        compiler_params=pltpu.CompilerParams(vmem_limit_bytes=30 * 2**20),
    )(*operands, *biases, *([before] if aliased else []))


def near_device(videos, spatial_filter, temporal_filter, spatial_bias, temporal_bias):
    shape = videos.shape[2:]
    height = shape[0]
    video = videos.reshape(shape)
    biases = [spatial_bias.reshape(1, -1), temporal_bias.reshape(1, -1)]
    tiles = lax.axis_size("tile")
    _, _, core = seat()
    depth = spatial_filter.shape[1]
    small, large = piece_rows(depth)
    starts = piece_starts(depth)
    swap = [(0, 1), (1, 0)]
    mates = [(i, i ^ 1) for i in range(tiles)]
    pairs = [(i, i ^ 4) for i in range(tiles)]
    across = [pair for i in range(1, tiles - 1, 2) for pair in ((i, i + 1), (i + 1, i))]
    light = pl.CostEstimate(flops=1000, bytes_accessed=1000, transcendentals=0)

    rows = 8
    sent = height - rows + 1
    a_y = lax.ppermute(lax.dynamic_slice_in_dim(spatial_filter, starts[0], small, axis=1), "dp", swap)
    b_y = lax.ppermute(lax.dynamic_slice_in_dim(spatial_filter, starts[4], large, axis=1), "dp", swap)
    far = lax.ppermute(video[:sent], "tile", across)
    a_z = lax.ppermute(a_y, "tile", pairs)
    base = base_call(video, spatial_filter, rows, light)
    a_y, a_z, b_y, base = lax.optimization_barrier((a_y, a_z, b_y, base))
    pieces = [a_y, a_z, *(lax.ppermute(part, "tile", mates) for part in (a_y, a_z)), b_y]
    pieces.append(lax.ppermute(b_y, "tile", mates))
    part = temporal_filter.shape[1] // 2
    c_y = lax.ppermute(lax.dynamic_slice_in_dim(temporal_filter, core * part, part, axis=1), "dp", swap)
    temporal_parts = [temporal_filter, c_y, lax.ppermute(c_y, "tile", mates)]
    spatial_parts = [spatial_filter, *pieces]

    own = own_call(video, base, biases[0], pieces, depth, rows, light)
    mate = [lax.ppermute(block, "tile", mates) for block in own]
    last = lax.ppermute(own[-1], "tile", across)
    out = mix_call(
        shape, own[:-1], mate[:-1], [far], False, temporal_parts, spatial_parts, biases, None, 0, rows, tiles, light
    )
    out = mix_call(
        shape, own[-1:], mate[-1:], [last], True, temporal_parts, [], biases, out, height - rows, rows, tiles, light
    )
    return out.reshape(videos.shape)


def padded_2(block, sides, width):
    for axis, dim in sides:
        count = lax.axis_size(axis)
        forward = [(i, i + 1) for i in range(count - 1)]
        backward = [(target, source) for source, target in forward]
        low = lax.ppermute(
            lax.slice_in_dim(block, block.shape[dim] - width, None, axis=dim), axis, forward
        )
        high = lax.ppermute(lax.slice_in_dim(block, 0, width, axis=dim), axis, backward)
        block = jnp.concatenate([low, block, high], axis=dim)
    return block


def spatial_term(padded, weight_piece):
    width = weight_piece.shape[1]
    height = padded.shape[2] - 2
    breadth = padded.shape[3] - 2
    columns = jnp.concatenate(
        [
            padded[:, :, row_off : row_off + height, col_off : col_off + breadth, :]
            for row_off in range(3)
            for col_off in range(3)
        ],
        axis=4,
    )
    matrix = weight_piece.reshape(9 * width, weight_piece.shape[2])
    return jnp.dot(columns.reshape(-1, 9 * width), matrix, preferred_element_type=jnp.float32)


def temporal_term(framed, weight_piece):
    width = weight_piece.shape[1]
    frames = framed.shape[1] - 2
    columns = jnp.concatenate([framed[:, lag : lag + frames] for lag in range(3)], axis=4)
    matrix = weight_piece.reshape(3 * width, weight_piece.shape[2])
    return jnp.dot(columns.reshape(-1, 3 * width), matrix, preferred_element_type=jnp.float32)


def any_device(videos, spatial_filter, temporal_filter, spatial_bias, temporal_bias):
    samples, frames, height, breadth, channels = videos.shape
    padded = jnp.pad(videos, ((0, 0), (0, 0), (1, 1), (1, 1), (0, 0)))
    summed = spatial_term(padded, lax.all_gather(spatial_filter, "dp", axis=1, tiled=True))
    activated = jax.nn.silu(summed + spatial_bias).astype(jnp.bfloat16)
    hidden = activated.reshape(samples, frames, height, breadth, channels)
    framed = padded_2(hidden, (("tile", 1),), 1)
    result = temporal_term(framed, lax.all_gather(temporal_filter, "dp", axis=1, tiled=True))
    return (result + temporal_bias).astype(jnp.bfloat16).reshape(videos.shape)


def per_device(videos, *rest):
    near = (
        videos.shape[0] == 1
        and videos.shape[1] == 1
        and videos.shape[2] % 32 == 0
        and lax.axis_size("dp") == 2
        and lax.axis_size("tile") % 8 == 0
    )
    return (near_device if near else any_device)(videos, *rest)


def solution(mesh):
    return jax.shard_map(
        per_device,
        mesh=mesh,
        in_specs=(
            P("dp", "tile", None, None, None),
            P(None, "dp", None),
            P(None, "dp", None),
            P(),
            P(),
        ),
        out_specs=P("dp", "tile", None, None, None),
        check_vma=False,
    )
```

```python
import functools

import jax
import jax.numpy as jnp
from jax import lax
from jax.experimental import pallas as pl
from jax.experimental.pallas import tpu as pltpu
from jax.sharding import PartitionSpec as P

ANY = pl.BlockSpec(memory_space=pltpu.HBM)


def dot(a, b):
    return jnp.dot(a, b, preferred_element_type=jnp.float32)


def silu(v):
    return v / (1 + jnp.exp(-v))


def halves(width):
    cut = width // 2
    return [slice(0, cut), slice(cut, width)]


def seat():
    return lax.axis_index("dp"), lax.rem(lax.axis_index("tile"), 2)


def half_starts(depth):
    _, core = seat()
    return [core * (depth // 2), (1 - core) * (depth // 2)]


def aligned(start):
    return pl.multiple_of(start, 16)


def rows_conv(padded, weights, taps, first, rows, breadth, columns):
    count = rows * breadth
    place = lax.rem(lax.broadcasted_iota(jnp.int32, (count, 1), 0), breadth)
    depth = padded.shape[2]
    lines = [padded[pl.ds(first + dy, rows)].reshape(count, depth) for dy in range(3)]

    def side(dx):
        mine = [(n, tap // 3) for n, tap in enumerate(taps) if tap % 3 == dx]
        matrix = jnp.concatenate([weights[n, :, columns] for n, _ in mine], axis=0)
        return dot(jnp.concatenate([lines[dy] for _, dy in mine], axis=1), matrix)

    total = side(1)
    total += jnp.where(place == 0, 0.0, pltpu.roll(side(0), 1, 0))
    total += jnp.where(place == breadth - 1, 0.0, pltpu.roll(side(2), count - 1, 0))
    return total


def cut_kernel(cuts, *refs):
    sources, targets, sem = refs[: len(cuts)], refs[len(cuts) : -1], refs[-1]
    copies = []
    for source, parts in zip(sources, cuts, strict=True):
        for where, _ in parts:
            n = len(copies)
            copies.append(pltpu.make_async_copy(source.at[where()], targets[n], sem.at[n]))
    for copy in copies:
        copy.start()
    for copy in copies:
        copy.wait()


def cut_call(sources, cuts, cost):
    shapes = [
        pltpu.VMEM(shape, source.dtype)
        for source, parts in zip(sources, cuts, strict=True)
        for _, shape in parts
    ]
    return pl.pallas_call(
        functools.partial(cut_kernel, cuts),
        in_specs=[ANY] * len(sources),
        out_specs=[pl.BlockSpec(memory_space=pltpu.VMEM)] * len(shapes),
        scratch_shapes=[pltpu.SemaphoreType.DMA((len(shapes),))],
        out_shape=shapes,
        cost_estimate=cost,
    )(*sources)


def conv_kernel(rows, block, taps, held, has_base, last, video, *refs):
    refs = list(refs)
    base = refs.pop(0) if has_base else None
    bias = refs.pop(0) if last else None
    pieces = 1 if held else 2
    height, breadth = video.shape[:2]
    steps = height // rows
    padded, weights, hidden, video_sem, part_sem, out_sem = refs[-6:]
    blocks = height // block
    outs = refs[-6 - (blocks if last else 1) : -6]
    parts = refs[: -6 - len(outs)]
    depth = weights.shape[1]
    i = pl.program_id(0)
    group, _ = seat()
    starts = [0] if held else half_starts(depth)

    def video_copy(j):
        channels = pl.ds(pl.multiple_of((group if held else 1 - group) * depth, 128), depth)
        return pltpu.make_async_copy(
            video.at[pl.ds(j * rows, rows), :, channels],
            padded.at[pl.ds(j * rows + 1, rows)],
            video_sem.at[j],
        )

    def part_copies():
        copies = []
        at = 0
        for n in range(0, len(parts), pieces):
            size = parts[n].shape[0]
            for p, start in enumerate(starts):
                there = weights.at[pl.ds(at, size), pl.ds(aligned(start), parts[n + p].shape[1])]
                copies.append(pltpu.make_async_copy(parts[n + p], there, part_sem.at[n + p]))
            at += size
        return copies

    def out_copy(j):
        return pltpu.make_async_copy(hidden.at[pl.ds(j * block, block)], outs[j], out_sem.at[j])

    @pl.when(i == 0)
    def _():
        video_copy(0).start()
        for copy in part_copies():
            copy.start()
        for j in range(1, steps):
            video_copy(j).start()
        padded[0] = jnp.zeros(padded.shape[1:], padded.dtype)
        padded[height + 1] = jnp.zeros(padded.shape[1:], padded.dtype)
        video_copy(0).wait()
        for copy in part_copies():
            copy.wait()

    @pl.when(i + 1 < steps)
    def _():
        video_copy(i + 1).wait()

    for columns in halves(weights.shape[2]):
        total = rows_conv(padded, weights, taps, i * rows, rows, breadth, columns)
        if has_base:
            total += base[:, :, columns].reshape(total.shape)
        if last:
            total = silu(total + bias[:, columns])
            hidden[pl.ds(i * rows, rows), :, columns] = total.astype(hidden.dtype).reshape(rows, breadth, -1)
        else:
            outs[0][:, :, columns] = total.reshape(rows, breadth, -1)

    if last:
        for j in range(blocks):

            @pl.when(i == ((j + 1) * block - 1) // rows)
            def _():
                out_copy(j).start()

        @pl.when(i == steps - 1)
        def _():
            for j in range(blocks):
                out_copy(j).wait()


def conv_call(video, base, bias, parts, depth, taps, held, rows, block, cost):
    height, breadth, _ = video.shape
    width = parts[0].shape[2]
    steps = height // rows
    last = bias is not None
    blocks = height // block
    lines = pl.BlockSpec((rows, breadth, width), lambda i: (i, 0, 0))
    specs, operands = [ANY], [video]
    if base is not None:
        specs, operands = specs + [lines], operands + [base]
    if last:
        specs, operands = specs + [pl.BlockSpec((1, width), lambda i: (0, 0))], operands + [bias]
    return pl.pallas_call(
        functools.partial(conv_kernel, rows, block, taps, held, base is not None, last),
        grid=(steps,),
        in_specs=specs + [ANY] * len(parts),
        out_specs=[ANY] * blocks if last else lines,
        scratch_shapes=[
            pltpu.VMEM((height + 2, breadth, depth), video.dtype),
            pltpu.VMEM((len(taps), depth, width), video.dtype),
            pltpu.VMEM((height, breadth, width) if last else (8, 128), video.dtype),
            pltpu.SemaphoreType.DMA((steps,)),
            pltpu.SemaphoreType.DMA((len(parts),)),
            pltpu.SemaphoreType.DMA((blocks,)),
        ],
        out_shape=[jax.ShapeDtypeStruct((block, breadth, width), video.dtype)] * blocks
        if last
        else jax.ShapeDtypeStruct((height, breadth, width), jnp.float32),
        cost_estimate=cost,
        compiler_params=pltpu.CompilerParams(vmem_limit_bytes=32 * 2**20),
    )(*operands, *parts)


def mix_kernel(rows, begin, blocks, given, pieces, aliased, tiles, *refs):
    refs = list(refs)

    def take(count):
        taken = refs[:count]
        del refs[:count]
        return taken

    steps = pl.num_programs(0)
    fars = take(blocks if given else 1)
    owns, mates = take(blocks), take(blocks)
    temporal_parts = take(1 + pieces[1])
    spatial_parts = [] if given else take(1 + pieces[0])
    spatial_bias, temporal_bias = take(2)
    take(aliased)
    (out,) = take(1)
    own, mate, far, temporal, spatial, row_sem, mate_sem, far_sem, temporal_sem, spatial_sem = refs
    breadth, width = out.shape[1:]
    depth = temporal.shape[1]
    group, core = seat()
    tile = lax.axis_index("tile")
    present = jnp.where(core == 0, tile > 0, tile < tiles - 1)
    i = pl.program_id(0)

    def part_copies(parts, weights, sem):
        held = parts[0].shape[1]
        copies = [
            pltpu.make_async_copy(parts[0], weights.at[:, pl.ds(aligned(group * held), held)], sem.at[0])
        ]
        at = 0
        for n in range(1, len(parts), 2):
            size = parts[n].shape[0]
            for p, start in enumerate(half_starts(held)):
                there = pl.ds(aligned((1 - group) * held + start), held // 2)
                copies.append(
                    pltpu.make_async_copy(parts[n + p], weights.at[pl.ds(at, size), there], sem.at[n + p])
                )
            at += size
        return copies

    def block_copies(sources, target, sem):
        return [
            pltpu.make_async_copy(source, target.at[pl.ds(p * source.shape[0], source.shape[0])], sem.at[p])
            for p, source in enumerate(sources)
        ]

    def far_copies():
        if given:
            return block_copies(fars, far, far_sem)
        low = begin - 1
        start, end = max(low, 0), min(low + far.shape[0], fars[0].shape[0])
        return [
            pltpu.make_async_copy(
                fars[0].at[pl.ds(start, end - start)], far.at[pl.ds(start - low, end - start)], far_sem.at[0]
            )
        ]

    first = part_copies(temporal_parts, temporal, temporal_sem)
    first += block_copies(owns, own, row_sem) + block_copies(mates, mate, mate_sem)
    second = far_copies() + ([] if given else part_copies(spatial_parts, spatial, spatial_sem))

    @pl.when(i == 0)
    def _():
        for copy in first + second:
            copy.start()
        if not given and begin == 0:
            far[0] = jnp.zeros(far.shape[1:], far.dtype)
        for copy in first:
            copy.wait()

    count = rows * breadth
    here = pl.ds(i * rows, rows)
    own_lines = own[here].reshape(count, depth)
    mate_lines = mate[here].reshape(count, depth)
    mate_tap, far_tap = 2 - 2 * core, 2 * core
    totals = [
        dot(own_lines, temporal[1, :, columns]) + dot(mate_lines, temporal[mate_tap, :, columns])
        for columns in halves(width)
    ]

    @pl.when(i == 0)
    def _():
        for copy in second:
            copy.wait()

    if given:
        far_lines = far[here].reshape(count, depth)
    else:
        far_lines = jnp.concatenate(
            [
                silu(
                    rows_conv(far, spatial, range(9), i * rows, rows, breadth, columns) + spatial_bias[:, columns]
                ).astype(far.dtype)
                for columns in halves(depth)
            ],
            axis=1,
        )
    far_lines = jnp.where(present, far_lines, jnp.zeros_like(far_lines))
    for total, columns in zip(totals, halves(width), strict=True):
        total += dot(far_lines, temporal[far_tap, :, columns]) + temporal_bias[:, columns]
        out[:, :, columns] = total.astype(out.dtype).reshape(rows, breadth, -1)


def mix_call(shape, owns, mates, fars, given, temporal_parts, spatial_parts, biases, before, begin, rows, tiles, cost):
    height, breadth, width = shape
    dtype = owns[0].dtype
    count = sum(own.shape[0] for own in owns)
    depth = owns[0].shape[2]
    aliased = 0 if before is None else 1
    operands = [*fars, *owns, *mates, *temporal_parts, *spatial_parts]
    whole = pl.BlockSpec((1, width), lambda i: (0, 0))
    pieces = (len(spatial_parts) - 1, len(temporal_parts) - 1)
    return pl.pallas_call(
        functools.partial(mix_kernel, rows, begin, len(owns), given, pieces, aliased, tiles),
        grid=(count // rows,),
        in_specs=[ANY] * len(operands) + [whole, whole] + [ANY] * aliased,
        out_specs=pl.BlockSpec((rows, breadth, width), lambda i: (i + begin // rows, 0, 0)),
        scratch_shapes=[
            pltpu.VMEM((count, breadth, depth), dtype),
            pltpu.VMEM((count, breadth, depth), dtype),
            pltpu.VMEM((count if given else count + 2, breadth, depth), dtype),
            pltpu.VMEM((3, depth, width), dtype),
            pltpu.VMEM((8, 128) if given else (9, depth, depth), dtype),
            pltpu.SemaphoreType.DMA((len(owns),)),
            pltpu.SemaphoreType.DMA((len(owns),)),
            pltpu.SemaphoreType.DMA((len(fars),)),
            pltpu.SemaphoreType.DMA((len(temporal_parts),)),
            pltpu.SemaphoreType.DMA((max(len(spatial_parts), 1),)),
        ],
        out_shape=jax.ShapeDtypeStruct(shape, dtype),
        input_output_aliases={len(operands) + 2: 0} if aliased else {},
        cost_estimate=cost,
        compiler_params=pltpu.CompilerParams(vmem_limit_bytes=40 * 2**20),
    )(*operands, *biases, *([before] if aliased else []))


def near_device(videos, spatial_filter, temporal_filter, spatial_bias, temporal_bias):
    shape = videos.shape[2:]
    height, breadth, channels = shape
    video = videos.reshape(shape)
    biases = [spatial_bias.reshape(1, -1), temporal_bias.reshape(1, -1)]
    tiles = lax.axis_size("tile")
    depth, width = spatial_filter.shape[1:]
    half = depth // 2
    swap = [(0, 1), (1, 0)]
    mates = [(i, i ^ 1) for i in range(tiles)]
    across = [pair for i in range(1, tiles - 1, 2) for pair in ((i, i + 1), (i + 1, i))]
    light = pl.CostEstimate(flops=1000, bytes_accessed=1000, transcendentals=0)
    heavy = pl.CostEstimate(flops=10**12, bytes_accessed=1000, transcendentals=0)

    def mine(first, count):
        return lambda: (pl.ds(first, count), pl.ds(aligned(half_starts(depth)[0]), half))

    rows = 8
    sent = height - rows + 1
    taps = [(0, 3), (3, 2), (5, 4)]
    middle = taps[2][0]
    cuts = [
        [(mine(first, count), (count, half, width)) for first, count in taps],
        [(mine(0, 3), (3, half, width))],
        [(lambda: (pl.ds(0, sent),), (sent, breadth, channels))],
    ]
    *cut, c_y, far = cut_call([spatial_filter, temporal_filter, video], cuts, light)
    far = lax.ppermute(far, "tile", across)
    fetched = [lax.ppermute(piece, "dp", swap) for piece in cut]

    def both(pieces):
        return [half for piece in pieces for half in (piece, lax.ppermute(piece, "tile", mates))]

    base = conv_call(video, None, None, [spatial_filter], depth, range(9), True, 16, rows, light)
    *early, base = lax.optimization_barrier((*fetched[:2], base))
    early = both(early)
    base = conv_call(video, base, None, early, depth, range(middle), False, 16, rows, light)
    *late, base = lax.optimization_barrier((*fetched[2:], base))
    late = both(late)
    own = conv_call(video, base, biases[0], late, depth, range(middle, 9), False, 16, rows, light)
    temporal_parts = [temporal_filter, *both([lax.ppermute(c_y, "dp", swap)])]
    spatial_parts = [spatial_filter, *early, *late]

    last = lax.ppermute(own[-1], "tile", across)
    mate = [lax.ppermute(block, "tile", mates) for block in own]
    out = mix_call(
        shape, own[:-1], mate[:-1], [far], False, temporal_parts, spatial_parts, biases, None, 0, 12, tiles, heavy
    )
    out = mix_call(
        shape, own[-1:], mate[-1:], [last], True, temporal_parts, [], biases, out, height - rows, rows, tiles, light
    )
    return out.reshape(videos.shape)


def padded_2(block, sides, width):
    for axis, dim in sides:
        count = lax.axis_size(axis)
        forward = [(i, i + 1) for i in range(count - 1)]
        backward = [(target, source) for source, target in forward]
        low = lax.ppermute(
            lax.slice_in_dim(block, block.shape[dim] - width, None, axis=dim), axis, forward
        )
        high = lax.ppermute(lax.slice_in_dim(block, 0, width, axis=dim), axis, backward)
        block = jnp.concatenate([low, block, high], axis=dim)
    return block


def spatial_term(padded, weight_piece):
    width = weight_piece.shape[1]
    height = padded.shape[2] - 2
    breadth = padded.shape[3] - 2
    columns = jnp.concatenate(
        [
            padded[:, :, row_off : row_off + height, col_off : col_off + breadth, :]
            for row_off in range(3)
            for col_off in range(3)
        ],
        axis=4,
    )
    matrix = weight_piece.reshape(9 * width, weight_piece.shape[2])
    return jnp.dot(columns.reshape(-1, 9 * width), matrix, preferred_element_type=jnp.float32)


def temporal_term(framed, weight_piece):
    width = weight_piece.shape[1]
    frames = framed.shape[1] - 2
    columns = jnp.concatenate([framed[:, lag : lag + frames] for lag in range(3)], axis=4)
    matrix = weight_piece.reshape(3 * width, weight_piece.shape[2])
    return jnp.dot(columns.reshape(-1, 3 * width), matrix, preferred_element_type=jnp.float32)


def any_device(videos, spatial_filter, temporal_filter, spatial_bias, temporal_bias):
    samples, frames, height, breadth, channels = videos.shape
    padded = jnp.pad(videos, ((0, 0), (0, 0), (1, 1), (1, 1), (0, 0)))
    summed = spatial_term(padded, lax.all_gather(spatial_filter, "dp", axis=1, tiled=True))
    activated = jax.nn.silu(summed + spatial_bias).astype(jnp.bfloat16)
    hidden = activated.reshape(samples, frames, height, breadth, channels)
    framed = padded_2(hidden, (("tile", 1),), 1)
    result = temporal_term(framed, lax.all_gather(temporal_filter, "dp", axis=1, tiled=True))
    return (result + temporal_bias).astype(jnp.bfloat16).reshape(videos.shape)


def per_device(videos, *rest):
    near = (
        videos.shape[0] == 1
        and videos.shape[1] == 1
        and videos.shape[2] % 32 == 0
        and lax.axis_size("dp") == 2
        and lax.axis_size("tile") % 2 == 0
    )
    return (near_device if near else any_device)(videos, *rest)


def solution(mesh):
    return jax.shard_map(
        per_device,
        mesh=mesh,
        in_specs=(
            P("dp", "tile", None, None, None),
            P(None, "dp", None),
            P(None, "dp", None),
            P(),
            P(),
        ),
        out_specs=P("dp", "tile", None, None, None),
        check_vma=False,
    )
```

```python
import functools

import jax
import jax.numpy as jnp
from jax import lax
from jax.experimental import pallas as pl
from jax.experimental.pallas import tpu as pltpu
from jax.sharding import PartitionSpec as P

ANY = pl.BlockSpec(memory_space=pltpu.HBM)


def dot(a, b):
    return jnp.dot(a, b, preferred_element_type=jnp.float32)


def silu(v):
    return v / (1 + jnp.exp(-v))


def halves(width):
    cut = width // 2
    return [slice(0, cut), slice(cut, width)]


def seat():
    return lax.axis_index("dp"), lax.rem(lax.axis_index("tile"), 2)


def half_starts(depth):
    _, core = seat()
    return [core * (depth // 2), (1 - core) * (depth // 2)]


def relay_starts(size):
    pair = lax.rem(lax.axis_index("tile") // 4, 2)
    return [pair * size, (1 - pair) * size]


def aligned(start):
    return pl.multiple_of(start, 16)


def rows_conv(padded, weights, taps, first, rows, breadth, columns):
    count = rows * breadth
    place = lax.rem(lax.broadcasted_iota(jnp.int32, (count, 1), 0), breadth)
    depth = padded.shape[2]
    lines = [padded[pl.ds(first + dy, rows)].reshape(count, depth) for dy in range(3)]

    def side(dx):
        mine = [(n, tap // 3) for n, tap in enumerate(taps) if tap % 3 == dx]
        matrix = jnp.concatenate([weights[n, :, columns] for n, _ in mine], axis=0)
        return dot(jnp.concatenate([lines[dy] for _, dy in mine], axis=1), matrix)

    total = side(1)
    total += jnp.where(place == 0, 0.0, pltpu.roll(side(0), 1, 0))
    total += jnp.where(place == breadth - 1, 0.0, pltpu.roll(side(2), count - 1, 0))
    return total


def cut_kernel(cuts, *refs):
    sources, targets, sem = refs[: len(cuts)], refs[len(cuts) : -1], refs[-1]
    copies = []
    for source, parts in zip(sources, cuts, strict=True):
        for where, _ in parts:
            n = len(copies)
            copies.append(pltpu.make_async_copy(source.at[where()], targets[n], sem.at[n]))
    for copy in copies:
        copy.start()
    for copy in copies:
        copy.wait()


def cut_call(sources, cuts, cost):
    shapes = [
        pltpu.VMEM(shape, source.dtype)
        for source, parts in zip(sources, cuts, strict=True)
        for _, shape in parts
    ]
    return pl.pallas_call(
        functools.partial(cut_kernel, cuts),
        in_specs=[ANY] * len(sources),
        out_specs=[pl.BlockSpec(memory_space=pltpu.VMEM)] * len(shapes),
        scratch_shapes=[pltpu.SemaphoreType.DMA((len(shapes),))],
        out_shape=shapes,
        cost_estimate=cost,
    )(*sources)


def conv_kernel(rows, blocks, taps, held, has_base, last, video, *refs):
    refs = list(refs)
    base = refs.pop(0) if has_base else None
    bias = refs.pop(0) if last else None
    tail = refs.pop(0) if last else None
    pieces = 1 if held else 2
    height, breadth = video.shape[:2]
    steps = height // rows
    padded, weights, hidden, video_sem, part_sem, out_sem = refs[-6:]
    outs = refs[-6 - len(blocks) : -6] if last else refs[-7:-6]
    parts = refs[: -6 - len(outs)]
    depth = weights.shape[1]
    i = pl.program_id(0)
    group, _ = seat()
    starts = [0] if held else half_starts(depth)

    def video_copy(j):
        channels = pl.ds(pl.multiple_of((group if held else 1 - group) * depth, 128), depth)
        return pltpu.make_async_copy(
            video.at[pl.ds(j * rows, rows), :, channels],
            padded.at[pl.ds(j * rows + 1, rows)],
            video_sem.at[j],
        )

    def part_copies():
        copies = []
        sizes = [part.shape[0] for part in parts[::pieces]]
        begins = relay_starts(sizes[0]) if last else [sum(sizes[:n]) for n in range(len(sizes))]
        for n, (size, begin) in enumerate(zip(sizes, begins, strict=True)):
            for p, start in enumerate(starts):
                part = parts[n * pieces + p]
                there = weights.at[pl.ds(begin, size), pl.ds(aligned(start), part.shape[1])]
                copies.append(pltpu.make_async_copy(part, there, part_sem.at[n * pieces + p]))
        return copies

    def out_copy(j):
        there = outs[j].at[pl.ds(0, blocks[j])]
        return pltpu.make_async_copy(hidden.at[pl.ds(sum(blocks[:j]), blocks[j])], there, out_sem.at[j])

    if last:
        lines = tail.shape[0]
        tail_in = pltpu.make_async_copy(tail, hidden.at[pl.ds(height, lines)], out_sem.at[len(blocks)])
        there = outs[-2].at[pl.ds(blocks[-2], lines)]
        tail_out = pltpu.make_async_copy(hidden.at[pl.ds(height, lines)], there, out_sem.at[len(blocks)])

    @pl.when(i == 0)
    def _():
        video_copy(0).start()
        if last:
            tail_in.start()
        for copy in part_copies():
            copy.start()
        for j in range(1, steps):
            video_copy(j).start()
        padded[0] = jnp.zeros(padded.shape[1:], padded.dtype)
        padded[height + 1] = jnp.zeros(padded.shape[1:], padded.dtype)
        video_copy(0).wait()
        for copy in part_copies():
            copy.wait()

    @pl.when(i + 1 < steps)
    def _():
        video_copy(i + 1).wait()

    for columns in halves(weights.shape[2]):
        total = rows_conv(padded, weights, taps, i * rows, rows, breadth, columns)
        if has_base:
            total += base[:, :, columns].reshape(total.shape)
        if last:
            total = silu(total + bias[:, columns])
            hidden[pl.ds(i * rows, rows), :, columns] = total.astype(hidden.dtype).reshape(rows, breadth, -1)
        else:
            outs[0][:, :, columns] = total.reshape(rows, breadth, -1)

    if last:
        for j in range(len(blocks)):

            @pl.when(i == (sum(blocks[: j + 1]) - 1) // rows)
            def _():
                out_copy(j).start()

        @pl.when(i == 0)
        def _():
            tail_in.wait()
            tail_out.start()

        @pl.when(i == steps - 1)
        def _():
            tail_out.wait()
            for j in range(len(blocks)):
                out_copy(j).wait()


def conv_call(video, base, bias, tail, parts, depth, taps, held, rows, blocks, cost):
    height, breadth, _ = video.shape
    width = parts[0].shape[2]
    steps = height // rows
    last = bias is not None
    lines = pl.BlockSpec((rows, breadth, width), lambda i: (i, 0, 0))
    specs, operands = [ANY], [video]
    if base is not None:
        specs, operands = specs + [lines], operands + [base]
    if last:
        specs, operands = specs + [pl.BlockSpec((1, width), lambda i: (0, 0)), ANY], operands + [bias, tail]
        extra = [0] * (len(blocks) - 2) + [tail.shape[0], 0]
    return pl.pallas_call(
        functools.partial(conv_kernel, rows, blocks, taps, held, base is not None, last),
        grid=(steps,),
        in_specs=specs + [ANY] * len(parts),
        out_specs=[ANY] * len(blocks) if last else lines,
        scratch_shapes=[
            pltpu.VMEM((height + 2, breadth, depth), video.dtype),
            pltpu.VMEM((len(taps), depth, width), video.dtype),
            pltpu.VMEM((height + tail.shape[0], breadth, width) if last else (16, 128), video.dtype),
            pltpu.SemaphoreType.DMA((steps,)),
            pltpu.SemaphoreType.DMA((len(parts),)),
            pltpu.SemaphoreType.DMA((len(blocks) + 1,)),
        ],
        out_shape=[
            jax.ShapeDtypeStruct((block + more, breadth, width), video.dtype)
            for block, more in zip(blocks, extra, strict=True)
        ]
        if last
        else jax.ShapeDtypeStruct((height, breadth, width), jnp.float32),
        cost_estimate=cost,
        compiler_params=pltpu.CompilerParams(vmem_limit_bytes=32 * 2**20),
    )(*operands, *parts)


def mix_kernel(rows, begin, sizes, given, parts, tiles, *refs):
    refs = list(refs)

    def take(count):
        taken = refs[:count]
        del refs[:count]
        return taken

    blocks = len(sizes)
    owns, mates = take(blocks), take(blocks)
    (far_part,) = take(1)
    temporal_parts = take(1 if given else 2)
    spatial_parts = take(parts)
    spatial_bias, temporal_bias = take(2)
    take(1 if given else 0)
    (out,) = take(1)
    (temporal,) = temporal_parts if given else take(1)
    own, mate, far, spatial, row_sem, mate_sem, far_sem, spatial_sem = refs
    breadth, width = out.shape[1:]
    depth = temporal.shape[1]
    group, core = seat()
    tile = lax.axis_index("tile")
    present = jnp.where(core == 0, tile > 0, tile < tiles - 1)
    i = pl.program_id(0)

    def spatial_copies():
        held = spatial_parts[0].shape[1]
        there = spatial.at[:, pl.ds(aligned(group * held), held)]
        copies = [pltpu.make_async_copy(spatial_parts[0], there, spatial_sem.at[0])]
        counts = [part.shape[0] for part in spatial_parts[1::2]]
        begins = [sum(counts[:n]) for n in range(len(counts))]
        begins[-2:] = [begins[-2] + start for start in relay_starts(counts[-1])]
        for n, (count, first) in enumerate(zip(counts, begins, strict=True)):
            for p, start in enumerate(half_starts(held)):
                at = 2 * n + p + 1
                there = spatial.at[pl.ds(first, count), pl.ds(aligned((1 - group) * held + start), held // 2)]
                copies.append(pltpu.make_async_copy(spatial_parts[at], there, spatial_sem.at[at]))
        return copies

    def block_copies(sources, target, sem):
        return [
            pltpu.make_async_copy(
                source.at[pl.ds(0, size)], target.at[pl.ds(sum(sizes[:p]), size)], sem.at[p]
            )
            for p, (source, size) in enumerate(zip(sources, sizes, strict=True))
        ]

    first = []
    if given:
        first = block_copies(owns, own, row_sem) + block_copies(mates, mate, mate_sem)
        second = [pltpu.make_async_copy(far_part, far, far_sem)]
    else:
        second = [pltpu.make_async_copy(far_part, far.at[pl.ds(1, far_part.shape[0])], far_sem)]
        second += spatial_copies()

    @pl.when(i == 0)
    def _():
        for copy in first + second:
            copy.start()
        if not given:
            far[0] = jnp.zeros(far.shape[1:], far.dtype)
        for copy in first:
            copy.wait()

    count = rows * breadth
    here = pl.ds(i * rows, rows)
    if not given:

        @pl.when(i == 0)
        def _():
            local, mine = temporal_parts
            held, part = depth // 2, depth // 4
            there = (1 - group) * held
            temporal[:, pl.ds(aligned(group * held), held)] = local[...]
            temporal[:, pl.ds(aligned(there + core * part), part)] = mine[...]
            tail = mates[-1][sizes[-1] :].reshape(3, part, width)
            temporal[:, pl.ds(aligned(there + (1 - core) * part), part)] = tail

        for j in range(blocks):

            @pl.when(i == j)
            def _():
                own[...] = owns[j][:rows]
                mate[...] = mates[j][:rows]

        own_lines, mate_lines = (ref[...].reshape(count, depth) for ref in (own, mate))
    else:
        own_lines, mate_lines = (ref[here].reshape(count, depth) for ref in (own, mate))
    mate_tap, far_tap = 2 - 2 * core, 2 * core

    def matrix(tap, columns):
        return temporal[tap, :, columns]

    totals = [
        dot(own_lines, matrix(1, columns)) + dot(mate_lines, matrix(mate_tap, columns)) for columns in halves(width)
    ]

    @pl.when(i == 0)
    def _():
        for copy in second:
            copy.wait()

    if given:
        far_lines = far[here].reshape(count, depth)
    else:
        far_lines = jnp.concatenate(
            [
                silu(
                    rows_conv(far, spatial, range(9), i * rows, rows, breadth, columns) + spatial_bias[:, columns]
                ).astype(far.dtype)
                for columns in halves(depth)
            ],
            axis=1,
        )
    far_lines = jnp.where(present, far_lines, jnp.zeros_like(far_lines))
    for total, columns in zip(totals, halves(width), strict=True):
        total += dot(far_lines, matrix(far_tap, columns)) + temporal_bias[:, columns]
        out[:, :, columns] = total.astype(out.dtype).reshape(rows, breadth, -1)


def mix_call(shape, far, owns, mates, sizes, temporal_parts, spatial_parts, biases, before, begin, rows, tiles, cost):
    height, breadth, width = shape
    dtype = far.dtype
    count, depth = sum(sizes), far.shape[2]
    given = before is not None
    operands = [*owns, *mates, far, *temporal_parts, *spatial_parts]
    specs = [ANY] * len(operands)
    in_vmem = pl.BlockSpec(memory_space=pltpu.VMEM)
    if given:
        specs[-1] = in_vmem
    else:
        for n in (*range(2 * len(owns)), 2 * len(owns) + 1, 2 * len(owns) + 2):
            specs[n] = in_vmem
            operands[n] = pltpu.with_memory_space_constraint(operands[n], pltpu.VMEM)
    whole = pl.BlockSpec((1, width), lambda i: (0, 0))
    out_shape = [jax.ShapeDtypeStruct(shape, dtype)]
    out_specs = [pl.BlockSpec((rows, breadth, width), lambda i: (i + begin // rows, 0, 0))]
    if not given:
        out_shape.append(pltpu.VMEM((3, depth, width), dtype))
        out_specs.append(in_vmem)
    return pl.pallas_call(
        functools.partial(mix_kernel, rows, begin, sizes, given, len(spatial_parts), tiles),
        grid=(count // rows,),
        in_specs=specs + [whole, whole] + [ANY] * given,
        out_specs=out_specs,
        scratch_shapes=[
            pltpu.VMEM((rows, breadth, depth), dtype),
            pltpu.VMEM((rows, breadth, depth), dtype),
            pltpu.VMEM((count if given else count + 2, breadth, depth), dtype),
            pltpu.VMEM((16, 128) if given else (9, depth, depth), dtype),
            pltpu.SemaphoreType.DMA((len(owns),)),
            pltpu.SemaphoreType.DMA((len(owns),)),
            pltpu.SemaphoreType.DMA,
            pltpu.SemaphoreType.DMA((max(len(spatial_parts), 1),)),
        ],
        out_shape=out_shape,
        input_output_aliases={len(operands) + 2: 0} if given else {},
        cost_estimate=cost,
        compiler_params=pltpu.CompilerParams(vmem_limit_bytes=40 * 2**20),
    )(*operands, *biases, *([before] if given else []))


def near_device(videos, spatial_filter, temporal_filter, spatial_bias, temporal_bias):
    shape = videos.shape[2:]
    height, breadth, channels = shape
    video = videos.reshape(shape)
    biases = [spatial_bias.reshape(1, -1), temporal_bias.reshape(1, -1)]
    tiles = lax.axis_size("tile")
    depth, width = spatial_filter.shape[1:]
    half = depth // 2
    swap = [(0, 1), (1, 0)]
    mates = [(i, i ^ 1) for i in range(tiles)]
    pairs = [(i, i ^ 4) for i in range(tiles)]
    across = [pair for i in range(1, tiles - 1, 2) for pair in ((i, i + 1), (i + 1, i))]
    light = pl.CostEstimate(flops=1000, bytes_accessed=1000, transcendentals=0)
    heavy = pl.CostEstimate(flops=10**12, bytes_accessed=1000, transcendentals=0)

    def mine(first, count):
        return lambda: (pl.ds(first, count), pl.ds(aligned(half_starts(depth)[0]), half))

    def relayed():
        return mine(middle + relay_starts(relay)[0], relay)()

    unit = height // 32
    blocks = tuple(unit * block for block in (8, 8, 8, 8))
    sent = height - blocks[-1] + 1
    taps = [(0, 3), (3, 2)]
    middle, relay = 5, 2
    cuts = [
        [(mine(first, count), (count, half, width)) for first, count in taps] + [(relayed, (relay, half, width))],
        [(mine(0, 3), (3, half, width))],
        [(lambda: (pl.ds(0, sent),), (sent, breadth, channels))],
    ]
    *cut, c_y, far = cut_call([spatial_filter, temporal_filter, video], cuts, light)
    far = lax.ppermute(far, "tile", across)
    fetched = [lax.ppermute(piece, "dp", swap) for piece in cut]

    def both(pieces):
        return [half for piece in pieces for half in (piece, lax.ppermute(piece, "tile", mates))]

    base = conv_call(video, None, None, None, [spatial_filter], depth, range(9), True, 16, blocks, light)
    *early, base = lax.optimization_barrier((*fetched[:2], base))
    early = both(early)
    base = conv_call(video, base, None, None, early, depth, range(middle), False, 16, blocks, light)
    other = lax.ppermute(fetched[-1], "tile", pairs)
    *late, base = lax.optimization_barrier((fetched[-1], other, base))
    late = both(late)
    c_y = lax.ppermute(c_y, "dp", swap)
    tail = c_y.reshape(-1, breadth, width)
    own = conv_call(video, base, biases[0], tail, late, depth, range(middle, 9), False, 16, blocks, light)
    temporal_parts = [temporal_filter, c_y]
    spatial_parts = [spatial_filter, *early, *late]

    last = lax.ppermute(own[-1], "tile", across)
    mate = [lax.ppermute(block, "tile", mates) for block in own]
    out, temporal = mix_call(
        shape, far, own[:-1], mate[:-1], blocks[:-1], temporal_parts, spatial_parts, biases, None, 0, 8, tiles, heavy
    )
    (out,) = mix_call(
        shape, last, own[-1:], mate[-1:], blocks[-1:], [temporal], [], biases, out, sent - 1, blocks[-1], tiles, light
    )
    return out.reshape(videos.shape)


def padded_2(block, sides, width):
    for axis, dim in sides:
        count = lax.axis_size(axis)
        forward = [(i, i + 1) for i in range(count - 1)]
        backward = [(target, source) for source, target in forward]
        low = lax.ppermute(
            lax.slice_in_dim(block, block.shape[dim] - width, None, axis=dim), axis, forward
        )
        high = lax.ppermute(lax.slice_in_dim(block, 0, width, axis=dim), axis, backward)
        block = jnp.concatenate([low, block, high], axis=dim)
    return block


def spatial_term(padded, weight_piece):
    width = weight_piece.shape[1]
    height = padded.shape[2] - 2
    breadth = padded.shape[3] - 2
    columns = jnp.concatenate(
        [
            padded[:, :, row_off : row_off + height, col_off : col_off + breadth, :]
            for row_off in range(3)
            for col_off in range(3)
        ],
        axis=4,
    )
    matrix = weight_piece.reshape(9 * width, weight_piece.shape[2])
    return jnp.dot(columns.reshape(-1, 9 * width), matrix, preferred_element_type=jnp.float32)


def temporal_term(framed, weight_piece):
    width = weight_piece.shape[1]
    frames = framed.shape[1] - 2
    columns = jnp.concatenate([framed[:, lag : lag + frames] for lag in range(3)], axis=4)
    matrix = weight_piece.reshape(3 * width, weight_piece.shape[2])
    return jnp.dot(columns.reshape(-1, 3 * width), matrix, preferred_element_type=jnp.float32)


def any_device(videos, spatial_filter, temporal_filter, spatial_bias, temporal_bias):
    samples, frames, height, breadth, channels = videos.shape
    padded = jnp.pad(videos, ((0, 0), (0, 0), (1, 1), (1, 1), (0, 0)))
    summed = spatial_term(padded, lax.all_gather(spatial_filter, "dp", axis=1, tiled=True))
    activated = jax.nn.silu(summed + spatial_bias).astype(jnp.bfloat16)
    hidden = activated.reshape(samples, frames, height, breadth, channels)
    framed = padded_2(hidden, (("tile", 1),), 1)
    result = temporal_term(framed, lax.all_gather(temporal_filter, "dp", axis=1, tiled=True))
    return (result + temporal_bias).astype(jnp.bfloat16).reshape(videos.shape)


def per_device(videos, spatial_filter, *rest):
    near = (
        videos.shape[0] == 1
        and videos.shape[1] == 1
        and videos.shape[2] % 32 == 0
        and spatial_filter.shape[1] % (2 * videos.shape[3]) == 0
        and lax.axis_size("dp") == 2
        and lax.axis_size("tile") % 8 == 0
    )
    return (near_device if near else any_device)(videos, spatial_filter, *rest)


def solution(mesh):
    return jax.shard_map(
        per_device,
        mesh=mesh,
        in_specs=(
            P("dp", "tile", None, None, None),
            P(None, "dp", None),
            P(None, "dp", None),
            P(),
            P(),
        ),
        out_specs=P("dp", "tile", None, None, None),
        check_vma=False,
    )
```

```python
import functools

import jax
import jax.numpy as jnp
from jax import lax
from jax.experimental import pallas as pl
from jax.experimental.pallas import tpu as pltpu
from jax.sharding import PartitionSpec as P

ANY = pl.BlockSpec(memory_space=pltpu.HBM)


def dot(a, b):
    return jnp.dot(a, b, preferred_element_type=jnp.float32)


def silu(v):
    return v / (1 + jnp.exp(-v))


def halves(width):
    cut = width // 2
    return [slice(0, cut), slice(cut, width)]


def seat():
    return lax.axis_index("dp"), lax.rem(lax.axis_index("tile"), 2)


def half_starts(depth):
    _, core = seat()
    return [core * (depth // 2), (1 - core) * (depth // 2)]


def relay_starts(size):
    pair = lax.rem(lax.axis_index("tile") // 4, 2)
    return [pair * size, (1 - pair) * size]


def aligned(start):
    return pl.multiple_of(start, 16)


def rows_conv(padded, weights, taps, first, rows, breadth, columns):
    count = rows * breadth
    place = lax.rem(lax.broadcasted_iota(jnp.int32, (count, 1), 0), breadth)
    depth = padded.shape[2]
    lines = [padded[pl.ds(first + dy, rows)].reshape(count, depth) for dy in range(3)]

    def side(dx):
        mine = [(n, tap // 3) for n, tap in enumerate(taps) if tap % 3 == dx]
        matrix = jnp.concatenate([weights(n, columns) for n, _ in mine], axis=0)
        return dot(jnp.concatenate([lines[dy] for _, dy in mine], axis=1), matrix)

    total = side(1)
    total += jnp.where(place == 0, 0.0, pltpu.roll(side(0), 1, 0))
    total += jnp.where(place == breadth - 1, 0.0, pltpu.roll(side(2), count - 1, 0))
    return total


def cut_kernel(cuts, *refs):
    sources, targets, sem = refs[: len(cuts)], refs[len(cuts) : -1], refs[-1]
    copies = []
    for source, parts in zip(sources, cuts, strict=True):
        for where, _ in parts:
            n = len(copies)
            copies.append(pltpu.make_async_copy(source.at[where()], targets[n], sem.at[n]))
    for copy in copies:
        copy.start()
    for copy in copies:
        copy.wait()


def cut_call(sources, cuts, cost):
    shapes = [
        pltpu.VMEM(shape, source.dtype)
        for source, parts in zip(sources, cuts, strict=True)
        for _, shape in parts
    ]
    return pl.pallas_call(
        functools.partial(cut_kernel, cuts),
        in_specs=[ANY] * len(sources),
        out_specs=[pl.BlockSpec(memory_space=pltpu.VMEM)] * len(shapes),
        scratch_shapes=[pltpu.SemaphoreType.DMA((len(shapes),))],
        out_shape=shapes,
        cost_estimate=cost,
    )(*sources)


def block_spans(blocks, step, rows):
    spans = []
    for j, size in enumerate(blocks):
        at = sum(blocks[:j])
        low, high = max(at, step * rows), min(at + size, (step + 1) * rows)
        if high > low:
            spans.append((j, slice(low - at, high - at), slice(low - step * rows, high - step * rows)))
    return spans


def conv_kernel(rows, taps, held, video, *refs):
    refs = list(refs)
    base = None if held else refs.pop(0)
    weights, video_sem, part_sem = refs[-3:]
    out, padded = refs[-5:-3]
    parts = refs[:-5]
    height, breadth = video.shape[:2]
    steps = height // rows
    depth = padded.shape[2]
    pieces = 1 if held else 2
    i = pl.program_id(0)
    group, _ = seat()
    starts = [0] if held else half_starts(depth)

    def video_copy(j):
        channels = pl.ds(pl.multiple_of((group if held else 1 - group) * depth, 128), depth)
        return pltpu.make_async_copy(
            video.at[pl.ds(j * rows, rows), :, channels],
            padded.at[pl.ds(j * rows + 1, rows)],
            video_sem.at[j],
        )

    def part_copies():
        copies, begin = [], 0
        for n in range(0, len(parts), pieces):
            size = parts[n].shape[0]
            for p, start in enumerate(starts):
                there = weights.at[pl.ds(begin, size), pl.ds(aligned(start), parts[n + p].shape[1])]
                copies.append(pltpu.make_async_copy(parts[n + p], there, part_sem.at[n + p]))
            begin += size
        return copies

    @pl.when(i == 0)
    def _():
        video_copy(0).start()
        for copy in part_copies():
            copy.start()
        for j in range(1, steps):
            video_copy(j).start()
        padded[0] = jnp.zeros(padded.shape[1:], padded.dtype)
        padded[height + 1] = jnp.zeros(padded.shape[1:], padded.dtype)
        video_copy(0).wait()
        for copy in part_copies():
            copy.wait()

    @pl.when(i + 1 < steps)
    def _():
        video_copy(i + 1).wait()

    for columns in halves(out.shape[2]):
        total = rows_conv(padded, lambda n, c: weights[n, :, c], taps, i * rows, rows, breadth, columns)
        here = pl.ds(i * rows, rows)
        if not held:
            total += base[here, :, columns].reshape(total.shape)
        out[here, :, columns] = total.reshape(rows, breadth, -1)


IN_VMEM = pl.BlockSpec(memory_space=pltpu.VMEM)


def in_vmem(array):
    return pltpu.with_memory_space_constraint(array, pltpu.VMEM)


def conv_call(video, base, parts, depth, taps, rows, cost):
    height, breadth, _ = video.shape
    width = parts[0].shape[2]
    steps = height // rows
    held = base is None
    padded = (height + 2, breadth, depth)
    return pl.pallas_call(
        functools.partial(conv_kernel, rows, taps, held),
        grid=(steps,),
        in_specs=[ANY] + [IN_VMEM] * (not held) + [ANY] * len(parts),
        out_specs=[IN_VMEM] * (1 if held else 2),
        scratch_shapes=[pltpu.VMEM(padded, video.dtype)] * held
        + [
            pltpu.VMEM((len(taps), depth, width), video.dtype),
            pltpu.SemaphoreType.DMA((steps,)),
            pltpu.SemaphoreType.DMA((len(parts),)),
        ],
        out_shape=[pltpu.VMEM((height, breadth, width), jnp.float32)]
        + [pltpu.VMEM(padded, video.dtype)] * (not held),
        cost_estimate=cost,
        compiler_params=pltpu.CompilerParams(vmem_limit_bytes=24 * 2**20),
    )(video, *([] if held else [in_vmem(base)]), *parts)


def own_kernel(rows, blocks, taps, padded, base, bias, tail, *refs):
    parts = refs[: -len(blocks) - 2]
    outs, whole, part_sem = refs[-len(blocks) - 2 : -2], refs[-2], refs[-1]
    local, early, late = parts[0], parts[1:-4], parts[-4:]
    breadth, depth = padded.shape[1:]
    steps = (padded.shape[0] - 2) // rows
    group, _ = seat()
    other = (1 - group) * depth

    def early_copies():
        there = whole.at[:, pl.ds(aligned(group * depth), depth)]
        copies, begin = [pltpu.make_async_copy(local, there, part_sem.at[0])], 0
        for n in range(0, len(early), 2):
            size = early[n].shape[0]
            for p, start in enumerate(half_starts(depth)):
                there = whole.at[pl.ds(begin, size), pl.ds(aligned(other + start), early[n + p].shape[1])]
                copies.append(pltpu.make_async_copy(early[n + p], there, part_sem.at[1 + n + p]))
            begin += size
        return copies

    for copy in early_copies():
        copy.start()
    for n, first in enumerate(relay_starts(late[0].shape[0])):
        for p, start in enumerate(half_starts(depth)):
            part = late[2 * n + p]
            for tap in range(part.shape[0]):
                whole[taps[0] + first + tap, pl.ds(aligned(other + start), part.shape[1])] = part[tap]
    outs[-2][blocks[-2] :] = tail[...]

    def matrix(n, columns):
        return whole[taps[n], pl.ds(aligned(other), depth), columns]

    for step in range(steps):
        for columns in halves(whole.shape[2]):
            total = rows_conv(padded, matrix, taps, step * rows, rows, breadth, columns)
            total += base[step * rows : (step + 1) * rows, :, columns].reshape(total.shape)
            hidden = silu(total + bias[:, columns]).astype(padded.dtype).reshape(rows, breadth, -1)
            for j, there, here in block_spans(blocks, step, rows):
                outs[j][there, :, columns] = hidden[here]

    for copy in early_copies():
        copy.wait()


def own_call(padded, base, bias, tail, parts, taps, rows, blocks, cost):
    height, breadth, depth = padded.shape[0] - 2, *padded.shape[1:]
    width = base.shape[2]
    sizes = [*blocks[:-2], blocks[-2] + tail.shape[0], blocks[-1]]
    operands = [padded, base, bias, tail, *parts]
    near_too = [n for n in range(len(operands)) if n < 4 or n >= len(operands) - 4]
    for n in near_too:
        operands[n] = in_vmem(operands[n])
    return pl.pallas_call(
        functools.partial(own_kernel, rows, blocks, taps),
        in_specs=[IN_VMEM if n in near_too else ANY for n in range(len(operands))],
        out_specs=[IN_VMEM] * (len(blocks) + 1),
        scratch_shapes=[pltpu.SemaphoreType.DMA((len(parts) - 4,))],
        out_shape=[pltpu.VMEM((size, breadth, width), padded.dtype) for size in sizes]
        + [pltpu.VMEM((9, 2 * depth, width), padded.dtype)],
        cost_estimate=cost,
        compiler_params=pltpu.CompilerParams(vmem_limit_bytes=24 * 2**20),
    )(*operands)


def mix_kernel(rows, begin, sizes, given, tiles, *refs):
    refs = list(refs)

    def take(count):
        taken = refs[:count]
        del refs[:count]
        return taken

    blocks = len(sizes)
    owns, mates = take(blocks), take(blocks)
    (far_part,) = take(1)
    temporal_parts = take(1 if given else 2)
    spatial = take(0 if given else 1)
    spatial_bias, temporal_bias = take(2)
    take(1 if given else 0)
    (out,) = take(1)
    (temporal,) = temporal_parts if given else take(1)
    own, mate, far, far_sem = refs
    breadth, width = out.shape[1:]
    depth = temporal.shape[1]
    group, core = seat()
    tile = lax.axis_index("tile")
    present = jnp.where(core == 0, tile > 0, tile < tiles - 1)
    i = pl.program_id(0)

    if given:
        second = []
        (own,), (mate,), far = owns, mates, far_part
    else:
        second = [pltpu.make_async_copy(far_part, far.at[pl.ds(1, far_part.shape[0])], far_sem)]

    @pl.when(i == 0)
    def _():
        for copy in second:
            copy.start()
        if not given:
            far[0] = jnp.zeros(far.shape[1:], far.dtype)

    count = rows * breadth
    here = pl.ds(i * rows, rows)
    if not given:

        @pl.when(i == 0)
        def _():
            local, mine = temporal_parts
            held, part = depth // 2, depth // 4
            there = (1 - group) * held
            temporal[:, pl.ds(aligned(group * held), held)] = local[...]
            temporal[:, pl.ds(aligned(there + core * part), part)] = mine[...]
            tail = mates[-1][sizes[-1] :].reshape(3, part, width)
            temporal[:, pl.ds(aligned(there + (1 - core) * part), part)] = tail

        for step in range(sum(sizes) // rows):

            @pl.when(i == step)
            def _():
                for j, there, here in block_spans(sizes, step, rows):
                    own[here], mate[here] = owns[j][there], mates[j][there]

        own_lines, mate_lines = (ref[...].reshape(count, depth) for ref in (own, mate))
    else:
        own_lines, mate_lines = (ref[here].reshape(count, depth) for ref in (own, mate))
    mate_tap, far_tap = 2 - 2 * core, 2 * core

    def matrix(tap, columns):
        return temporal[tap, :, columns]

    def spatial_rows(tap, columns):
        return spatial[0][tap, :, columns]

    def product(lines, taps, columns):
        return dot(jnp.concatenate(lines, axis=1), jnp.concatenate([matrix(tap, columns) for tap in taps], axis=0))

    def masked(lines):
        return jnp.where(present, lines, jnp.zeros_like(lines))

    def put(total, columns):
        total += temporal_bias[:, columns]
        out[:, :, columns] = total.astype(out.dtype).reshape(rows, breadth, -1)

    if given:
        lines = [own_lines, mate_lines, masked(far[here].reshape(count, depth))]
        for columns in halves(width):
            put(product(lines, (1, mate_tap, far_tap), columns), columns)
        return

    totals = [product([own_lines, mate_lines], (1, mate_tap), columns) for columns in halves(width)]

    @pl.when(i == 0)
    def _():
        for copy in second:
            copy.wait()

    far_lines = jnp.concatenate(
        [
            silu(
                rows_conv(far, spatial_rows, range(9), i * rows, rows, breadth, columns) + spatial_bias[:, columns]
            ).astype(far.dtype)
            for columns in halves(depth)
        ],
        axis=1,
    )
    far_lines = masked(far_lines)
    for total, columns in zip(totals, halves(width), strict=True):
        put(total + dot(far_lines, matrix(far_tap, columns)), columns)


def mix_call(shape, far, owns, mates, sizes, temporal_parts, spatial, biases, before, begin, rows, tiles, cost):
    height, breadth, width = shape
    dtype = far.dtype
    count, depth = sum(sizes), far.shape[2]
    given = before is not None
    operands = [*owns, *mates, far, *temporal_parts, *spatial]
    specs = [ANY] * len(operands)
    for n in range(len(operands)):
        if given or n != 2 * len(owns):
            specs[n] = IN_VMEM
            operands[n] = in_vmem(operands[n])
    out_shape = [jax.ShapeDtypeStruct(shape, dtype)]
    out_specs = [pl.BlockSpec((rows, breadth, width), lambda i: (i + begin // rows, 0, 0))]
    if not given:
        out_shape.append(pltpu.VMEM((3, depth, width), dtype))
        out_specs.append(IN_VMEM)
    return pl.pallas_call(
        functools.partial(mix_kernel, rows, begin, sizes, given, tiles),
        grid=(count // rows,),
        in_specs=specs + [IN_VMEM, IN_VMEM] + [ANY] * given,
        out_specs=out_specs,
        scratch_shapes=[
            pltpu.VMEM((16, 128) if given else (rows, breadth, depth), dtype),
            pltpu.VMEM((16, 128) if given else (rows, breadth, depth), dtype),
            pltpu.VMEM((16, 128) if given else (count + 2, breadth, depth), dtype),
            pltpu.SemaphoreType.DMA,
        ],
        out_shape=out_shape,
        input_output_aliases={len(operands) + 2: 0} if given else {},
        cost_estimate=cost,
        compiler_params=pltpu.CompilerParams(vmem_limit_bytes=40 * 2**20),
    )(*operands, *map(in_vmem, biases), *([before] if given else []))


def near_device(videos, spatial_filter, temporal_filter, spatial_bias, temporal_bias):
    shape = videos.shape[2:]
    height, breadth, channels = shape
    video = videos.reshape(shape)
    biases = [spatial_bias.reshape(1, -1), temporal_bias.reshape(1, -1)]
    tiles = lax.axis_size("tile")
    depth, width = spatial_filter.shape[1:]
    half = depth // 2
    swap = [(0, 1), (1, 0)]
    mates = [(i, i ^ 1) for i in range(tiles)]
    pairs = [(i, i ^ 4) for i in range(tiles)]
    across = [pair for i in range(1, tiles - 1, 2) for pair in ((i, i + 1), (i + 1, i))]
    light = pl.CostEstimate(flops=1000, bytes_accessed=1000, transcendentals=0)
    heavy = pl.CostEstimate(flops=10**12, bytes_accessed=1000, transcendentals=0)

    def mine(first, count):
        return lambda: (pl.ds(first, count), pl.ds(aligned(half_starts(depth)[0]), half))

    def relayed():
        return mine(middle + relay_starts(relay)[0], relay)()

    unit = height // 32
    blocks = tuple(unit * block for block in (8, 8, 8, 8))
    sent = height - blocks[-1] + 1
    taps = [(0, 3), (3, 2)]
    middle, relay = 5, 2
    cuts = [
        [(mine(first, count), (count, half, width)) for first, count in taps] + [(relayed, (relay, half, width))],
        [(mine(0, 3), (3, half, width))],
        [(lambda: (pl.ds(0, sent),), (sent, breadth, channels))],
    ]
    *cut, c_y, far = cut_call([spatial_filter, temporal_filter, video], cuts, light)
    far = lax.ppermute(far, "tile", across)
    fetched = [lax.ppermute(piece, "dp", swap) for piece in cut]

    def both(pieces):
        return [half for piece in pieces for half in (piece, lax.ppermute(piece, "tile", mates))]

    (base,) = conv_call(video, None, [spatial_filter], depth, range(9), 16, light)
    *early, base = lax.optimization_barrier((*fetched[:-1], base))
    early = both(early)
    base, padded = conv_call(video, base, early, depth, range(middle), 16, light)
    other = lax.ppermute(fetched[-1], "tile", pairs)
    *late, base = lax.optimization_barrier((fetched[-1], other, base))
    late = both(late)
    c_y = lax.ppermute(c_y, "dp", swap)
    tail = c_y.reshape(-1, breadth, width)
    parts = [spatial_filter, *early, *late]
    *own, spatial = own_call(padded, base, biases[0], tail, parts, range(middle, 9), 16, blocks, light)
    temporal_parts = [temporal_filter, c_y]

    last = lax.ppermute(own[-1], "tile", across)
    mate = [lax.ppermute(block, "tile", mates) for block in own]
    out, temporal = mix_call(
        shape, far, own[:-1], mate[:-1], blocks[:-1], temporal_parts, [spatial], biases, None, 0, 12, tiles, heavy
    )
    (out,) = mix_call(
        shape, last, own[-1:], mate[-1:], blocks[-1:], [temporal], [], biases, out, sent - 1, blocks[-1], tiles, light
    )
    return out.reshape(videos.shape)


def padded_2(block, sides, width):
    for axis, dim in sides:
        count = lax.axis_size(axis)
        forward = [(i, i + 1) for i in range(count - 1)]
        backward = [(target, source) for source, target in forward]
        low = lax.ppermute(
            lax.slice_in_dim(block, block.shape[dim] - width, None, axis=dim), axis, forward
        )
        high = lax.ppermute(lax.slice_in_dim(block, 0, width, axis=dim), axis, backward)
        block = jnp.concatenate([low, block, high], axis=dim)
    return block


def spatial_term(padded, weight_piece):
    width = weight_piece.shape[1]
    height = padded.shape[2] - 2
    breadth = padded.shape[3] - 2
    columns = jnp.concatenate(
        [
            padded[:, :, row_off : row_off + height, col_off : col_off + breadth, :]
            for row_off in range(3)
            for col_off in range(3)
        ],
        axis=4,
    )
    matrix = weight_piece.reshape(9 * width, weight_piece.shape[2])
    return jnp.dot(columns.reshape(-1, 9 * width), matrix, preferred_element_type=jnp.float32)


def temporal_term(framed, weight_piece):
    width = weight_piece.shape[1]
    frames = framed.shape[1] - 2
    columns = jnp.concatenate([framed[:, lag : lag + frames] for lag in range(3)], axis=4)
    matrix = weight_piece.reshape(3 * width, weight_piece.shape[2])
    return jnp.dot(columns.reshape(-1, 3 * width), matrix, preferred_element_type=jnp.float32)


def any_device(videos, spatial_filter, temporal_filter, spatial_bias, temporal_bias):
    samples, frames, height, breadth, channels = videos.shape
    padded = jnp.pad(videos, ((0, 0), (0, 0), (1, 1), (1, 1), (0, 0)))
    summed = spatial_term(padded, lax.all_gather(spatial_filter, "dp", axis=1, tiled=True))
    activated = jax.nn.silu(summed + spatial_bias).astype(jnp.bfloat16)
    hidden = activated.reshape(samples, frames, height, breadth, channels)
    framed = padded_2(hidden, (("tile", 1),), 1)
    result = temporal_term(framed, lax.all_gather(temporal_filter, "dp", axis=1, tiled=True))
    return (result + temporal_bias).astype(jnp.bfloat16).reshape(videos.shape)


def per_device(videos, spatial_filter, *rest):
    near = (
        videos.shape[0] == 1
        and videos.shape[1] == 1
        and videos.shape[2] % 32 == 0
        and spatial_filter.shape[1] % (2 * videos.shape[3]) == 0
        and lax.axis_size("dp") == 2
        and lax.axis_size("tile") % 8 == 0
    )
    return (near_device if near else any_device)(videos, spatial_filter, *rest)


def solution(mesh):
    return jax.shard_map(
        per_device,
        mesh=mesh,
        in_specs=(
            P("dp", "tile", None, None, None),
            P(None, "dp", None),
            P(None, "dp", None),
            P(),
            P(),
        ),
        out_specs=P("dp", "tile", None, None, None),
        check_vma=False,
    )
```

```python
import functools

import jax
import jax.numpy as jnp
from jax import lax
from jax.experimental import pallas as pl
from jax.experimental.pallas import tpu as pltpu
from jax.sharding import PartitionSpec as P

ANY = pl.BlockSpec(memory_space=pltpu.HBM)


def dot(a, b):
    return jnp.dot(a, b, preferred_element_type=jnp.float32)


def silu(v):
    return v / (1 + jnp.exp(-v))


def halves(width):
    cut = width // 2
    return [slice(0, cut), slice(cut, width)]


def seat():
    return lax.axis_index("dp"), lax.rem(lax.axis_index("tile"), 2)


def half_starts(depth):
    _, core = seat()
    return [core * (depth // 2), (1 - core) * (depth // 2)]


def relay_starts(size):
    pair = lax.rem(lax.axis_index("tile") // 4, 2)
    return [pair * size, (1 - pair) * size]


def aligned(start):
    return pl.multiple_of(start, 16)


def rows_conv(padded, weights, taps, first, rows, breadth, columns):
    count = rows * breadth
    place = lax.rem(lax.broadcasted_iota(jnp.int32, (count, 1), 0), breadth)
    depth = padded.shape[2]
    lines = [padded[pl.ds(first + dy, rows)].reshape(count, depth) for dy in range(3)]

    def side(dx):
        mine = [(n, tap // 3) for n, tap in enumerate(taps) if tap % 3 == dx]
        matrix = jnp.concatenate([weights(n, columns) for n, _ in mine], axis=0)
        return dot(jnp.concatenate([lines[dy] for _, dy in mine], axis=1), matrix)

    total = side(1)
    total += jnp.where(place == 0, 0.0, pltpu.roll(side(0), 1, 0))
    total += jnp.where(place == breadth - 1, 0.0, pltpu.roll(side(2), count - 1, 0))
    return total


def cut_kernel(cuts, *refs):
    sources, targets, sem = refs[: len(cuts)], refs[len(cuts) : -1], refs[-1]
    copies = []
    for source, parts in zip(sources, cuts, strict=True):
        for where, _ in parts:
            n = len(copies)
            copies.append(pltpu.make_async_copy(source.at[where()], targets[n], sem.at[n]))
    for copy in copies:
        copy.start()
    for copy in copies:
        copy.wait()


def cut_call(sources, cuts, cost):
    shapes = [
        pltpu.VMEM(shape, source.dtype)
        for source, parts in zip(sources, cuts, strict=True)
        for _, shape in parts
    ]
    return pl.pallas_call(
        functools.partial(cut_kernel, cuts),
        in_specs=[ANY] * len(sources),
        out_specs=[pl.BlockSpec(memory_space=pltpu.VMEM)] * len(shapes),
        scratch_shapes=[pltpu.SemaphoreType.DMA((len(shapes),))],
        out_shape=shapes,
        cost_estimate=cost,
    )(*sources)


def block_spans(blocks, step, rows):
    spans = []
    for j, size in enumerate(blocks):
        at = sum(blocks[:j])
        low, high = max(at, step * rows), min(at + size, (step + 1) * rows)
        if high > low:
            spans.append((j, slice(low - at, high - at), slice(low - step * rows, high - step * rows)))
    return spans


def conv_kernel(rows, taps, held, video, *refs):
    refs = list(refs)
    base = None if held else refs.pop(0)
    weights, video_sem, part_sem = refs[-3:]
    out, padded = refs[-5:-3]
    parts = refs[:-5]
    height, breadth = video.shape[:2]
    steps = height // rows
    depth = padded.shape[2]
    pieces = 1 if held else 2
    i = pl.program_id(0)
    group, _ = seat()
    starts = [0] if held else half_starts(depth)

    def video_copy(j):
        channels = pl.ds(pl.multiple_of((group if held else 1 - group) * depth, 128), depth)
        return pltpu.make_async_copy(
            video.at[pl.ds(j * rows, rows), :, channels],
            padded.at[pl.ds(j * rows + 1, rows)],
            video_sem.at[j],
        )

    def part_copies():
        copies, begin = [], 0
        for n in range(0, len(parts), pieces):
            size = parts[n].shape[0]
            for p, start in enumerate(starts):
                there = weights.at[pl.ds(begin, size), pl.ds(aligned(start), parts[n + p].shape[1])]
                copies.append(pltpu.make_async_copy(parts[n + p], there, part_sem.at[n + p]))
            begin += size
        return copies

    @pl.when(i == 0)
    def _():
        video_copy(0).start()
        for copy in part_copies():
            copy.start()
        for j in range(1, steps):
            video_copy(j).start()
        padded[0] = jnp.zeros(padded.shape[1:], padded.dtype)
        padded[height + 1] = jnp.zeros(padded.shape[1:], padded.dtype)
        video_copy(0).wait()
        for copy in part_copies():
            copy.wait()

    @pl.when(i + 1 < steps)
    def _():
        video_copy(i + 1).wait()

    for columns in halves(out.shape[2]):
        total = rows_conv(padded, lambda n, c: weights[n, :, c], taps, i * rows, rows, breadth, columns)
        here = pl.ds(i * rows, rows)
        if not held:
            total += base[here, :, columns].reshape(total.shape)
        out[here, :, columns] = total.reshape(rows, breadth, -1)


IN_VMEM = pl.BlockSpec(memory_space=pltpu.VMEM)


def in_vmem(array):
    return pltpu.with_memory_space_constraint(array, pltpu.VMEM)


def conv_call(video, base, parts, depth, taps, rows, cost):
    height, breadth, _ = video.shape
    width = parts[0].shape[2]
    steps = height // rows
    held = base is None
    padded = (height + 2, breadth, depth)
    return pl.pallas_call(
        functools.partial(conv_kernel, rows, taps, held),
        grid=(steps,),
        in_specs=[ANY] + [IN_VMEM] * (not held) + [ANY] * len(parts),
        out_specs=[IN_VMEM] * (1 if held else 2),
        scratch_shapes=[pltpu.VMEM(padded, video.dtype)] * held
        + [
            pltpu.VMEM((len(taps), depth, width), video.dtype),
            pltpu.SemaphoreType.DMA((steps,)),
            pltpu.SemaphoreType.DMA((len(parts),)),
        ],
        out_shape=[pltpu.VMEM((height, breadth, width), jnp.float32)]
        + [pltpu.VMEM(padded, video.dtype)] * (not held),
        cost_estimate=cost,
        compiler_params=pltpu.CompilerParams(vmem_limit_bytes=24 * 2**20),
    )(video, *([] if held else [in_vmem(base)]), *parts)


def own_kernel(rows, blocks, taps, padded, base, bias, tail, *refs):
    parts = refs[: -len(blocks) - 2]
    outs, whole, part_sem = refs[-len(blocks) - 2 : -2], refs[-2], refs[-1]
    local, early, late = parts[0], parts[1:-4], parts[-4:]
    breadth, depth = padded.shape[1:]
    steps = (padded.shape[0] - 2) // rows
    group, _ = seat()
    other = (1 - group) * depth

    def early_copies():
        there = whole.at[:, pl.ds(aligned(group * depth), depth)]
        copies, begin = [pltpu.make_async_copy(local, there, part_sem.at[0])], 0
        for n in range(0, len(early), 2):
            size = early[n].shape[0]
            for p, start in enumerate(half_starts(depth)):
                there = whole.at[pl.ds(begin, size), pl.ds(aligned(other + start), early[n + p].shape[1])]
                copies.append(pltpu.make_async_copy(early[n + p], there, part_sem.at[1 + n + p]))
            begin += size
        return copies

    for copy in early_copies():
        copy.start()
    for n, first in enumerate(relay_starts(late[0].shape[0])):
        for p, start in enumerate(half_starts(depth)):
            part = late[2 * n + p]
            for tap in range(part.shape[0]):
                whole[taps[0] + first + tap, pl.ds(aligned(other + start), part.shape[1])] = part[tap]
    outs[-2][blocks[-2] :] = tail[...]

    def matrix(n, columns):
        return whole[taps[n], pl.ds(aligned(other), depth), columns]

    for step in range(steps):
        for columns in halves(whole.shape[2]):
            total = rows_conv(padded, matrix, taps, step * rows, rows, breadth, columns)
            total += base[step * rows : (step + 1) * rows, :, columns].reshape(total.shape)
            hidden = silu(total + bias[:, columns]).astype(padded.dtype).reshape(rows, breadth, -1)
            for j, there, here in block_spans(blocks, step, rows):
                outs[j][there, :, columns] = hidden[here]

    for copy in early_copies():
        copy.wait()


def own_call(padded, base, bias, tail, parts, taps, rows, blocks, cost):
    height, breadth, depth = padded.shape[0] - 2, *padded.shape[1:]
    width = base.shape[2]
    sizes = [*blocks[:-2], blocks[-2] + tail.shape[0], blocks[-1]]
    operands = [padded, base, bias, tail, *parts]
    near_too = [n for n in range(len(operands)) if n < 4 or n >= len(operands) - 4]
    for n in near_too:
        operands[n] = in_vmem(operands[n])
    return pl.pallas_call(
        functools.partial(own_kernel, rows, blocks, taps),
        in_specs=[IN_VMEM if n in near_too else ANY for n in range(len(operands))],
        out_specs=[IN_VMEM] * (len(blocks) + 1),
        scratch_shapes=[pltpu.SemaphoreType.DMA((len(parts) - 4,))],
        out_shape=[pltpu.VMEM((size, breadth, width), padded.dtype) for size in sizes]
        + [pltpu.VMEM((9, 2 * depth, width), padded.dtype)],
        cost_estimate=cost,
        compiler_params=pltpu.CompilerParams(vmem_limit_bytes=24 * 2**20),
    )(*operands)


def mix_kernel(rows, begin, sizes, given, tiles, *refs):
    refs = list(refs)

    def take(count):
        taken = refs[:count]
        del refs[:count]
        return taken

    blocks = len(sizes)
    owns, mates = take(blocks), take(blocks)
    (far_part,) = take(1)
    temporal_parts = take(1 if given else 2)
    spatial = take(0 if given else 1)
    spatial_bias, temporal_bias = take(2)
    take(1 if given else 0)
    (out,) = take(1)
    (temporal,) = temporal_parts if given else take(1)
    own, mate, far, far_sem = refs
    breadth, width = out.shape[1:]
    depth = temporal.shape[1]
    group, core = seat()
    tile = lax.axis_index("tile")
    present = jnp.where(core == 0, tile > 0, tile < tiles - 1)
    i = pl.program_id(0)

    if given:
        second = []
        (own,), (mate,), far = owns, mates, far_part
    else:
        second = [pltpu.make_async_copy(far_part, far.at[pl.ds(1, far_part.shape[0])], far_sem)]

    @pl.when(i == 0)
    def _():
        for copy in second:
            copy.start()
        if not given:
            far[0] = jnp.zeros(far.shape[1:], far.dtype)

    count = rows * breadth
    here = pl.ds(i * rows, rows)
    if not given:

        @pl.when(i == 0)
        def _():
            local, mine = temporal_parts
            held, part = depth // 2, depth // 4
            there = (1 - group) * held
            temporal[:, pl.ds(aligned(group * held), held)] = local[...]
            temporal[:, pl.ds(aligned(there + core * part), part)] = mine[...]
            tail = mates[-1][sizes[-1] :].reshape(3, part, width)
            temporal[:, pl.ds(aligned(there + (1 - core) * part), part)] = tail

        for step in range(sum(sizes) // rows):

            @pl.when(i == step)
            def _():
                for j, there, here in block_spans(sizes, step, rows):
                    own[here], mate[here] = owns[j][there], mates[j][there]

        own_lines, mate_lines = (ref[...].reshape(count, depth) for ref in (own, mate))
    else:
        own_lines, mate_lines = (ref[here].reshape(count, depth) for ref in (own, mate))
    mate_tap, far_tap = 2 - 2 * core, 2 * core

    def matrix(tap, columns):
        return temporal[tap, :, columns]

    def spatial_rows(tap, columns):
        return spatial[0][tap, :, columns]

    def product(lines, taps, columns):
        return dot(jnp.concatenate(lines, axis=1), jnp.concatenate([matrix(tap, columns) for tap in taps], axis=0))

    def masked(lines):
        return jnp.where(present, lines, jnp.zeros_like(lines))

    def put(total, columns):
        total += temporal_bias[:, columns]
        out[:, :, columns] = total.astype(out.dtype).reshape(rows, breadth, -1)

    if given:
        lines = [own_lines, mate_lines, masked(far[here].reshape(count, depth))]
        for columns in halves(width):
            put(product(lines, (1, mate_tap, far_tap), columns), columns)
        return

    totals = [product([own_lines, mate_lines], (1, mate_tap), columns) for columns in halves(width)]

    @pl.when(i == 0)
    def _():
        for copy in second:
            copy.wait()

    far_lines = jnp.concatenate(
        [
            silu(
                rows_conv(far, spatial_rows, range(9), i * rows, rows, breadth, columns) + spatial_bias[:, columns]
            ).astype(far.dtype)
            for columns in halves(depth)
        ],
        axis=1,
    )
    far_lines = masked(far_lines)
    for total, columns in zip(totals, halves(width), strict=True):
        put(total + dot(far_lines, matrix(far_tap, columns)), columns)


def mix_call(shape, far, owns, mates, sizes, temporal_parts, spatial, biases, before, begin, rows, tiles, cost):
    height, breadth, width = shape
    dtype = far.dtype
    count, depth = sum(sizes), far.shape[2]
    given = before is not None
    operands = [*owns, *mates, far, *temporal_parts, *spatial]
    specs = [ANY] * len(operands)
    for n in range(len(operands)):
        if given or n != 2 * len(owns):
            specs[n] = IN_VMEM
            operands[n] = in_vmem(operands[n])
    out_shape = [jax.ShapeDtypeStruct(shape, dtype)]
    out_specs = [pl.BlockSpec((rows, breadth, width), lambda i: (i + begin // rows, 0, 0))]
    if not given:
        out_shape.append(pltpu.VMEM((3, depth, width), dtype))
        out_specs.append(IN_VMEM)
    return pl.pallas_call(
        functools.partial(mix_kernel, rows, begin, sizes, given, tiles),
        grid=(count // rows,),
        in_specs=specs + [IN_VMEM, IN_VMEM] + [ANY] * given,
        out_specs=out_specs,
        scratch_shapes=[
            pltpu.VMEM((16, 128) if given else (rows, breadth, depth), dtype),
            pltpu.VMEM((16, 128) if given else (rows, breadth, depth), dtype),
            pltpu.VMEM((16, 128) if given else (count + 2, breadth, depth), dtype),
            pltpu.SemaphoreType.DMA,
        ],
        out_shape=out_shape,
        input_output_aliases={len(operands) + 2: 0} if given else {},
        cost_estimate=cost,
        compiler_params=pltpu.CompilerParams(vmem_limit_bytes=40 * 2**20),
    )(*operands, *map(in_vmem, biases), *([before] if given else []))


def near_device(videos, spatial_filter, temporal_filter, spatial_bias, temporal_bias):
    shape = videos.shape[2:]
    height, breadth, channels = shape
    video = videos.reshape(shape)
    biases = [spatial_bias.reshape(1, -1), temporal_bias.reshape(1, -1)]
    tiles = lax.axis_size("tile")
    depth, width = spatial_filter.shape[1:]
    half = depth // 2
    swap = [(0, 1), (1, 0)]
    mates = [(i, i ^ 1) for i in range(tiles)]
    pairs = [(i, i ^ 4) for i in range(tiles)]
    across = [pair for i in range(1, tiles - 1, 2) for pair in ((i, i + 1), (i + 1, i))]
    light = pl.CostEstimate(flops=1000, bytes_accessed=1000, transcendentals=0)
    heavy = pl.CostEstimate(flops=10**12, bytes_accessed=1000, transcendentals=0)

    def mine(first, count):
        return lambda: (pl.ds(first, count), pl.ds(aligned(half_starts(depth)[0]), half))

    def relayed():
        return mine(middle + relay_starts(relay)[0], relay)()

    unit = height // 32
    blocks = tuple(unit * block for block in (9, 9, 6, 8))
    sent = height - blocks[-1] + 1
    taps = [(0, 3), (3, 2)]
    middle, relay = 5, 2
    cuts = [
        [(mine(first, count), (count, half, width)) for first, count in taps] + [(relayed, (relay, half, width))],
        [(mine(0, 3), (3, half, width))],
        [(lambda: (pl.ds(0, sent),), (sent, breadth, channels))],
    ]
    *cut, c_y, far = cut_call([spatial_filter, temporal_filter, video], cuts, light)
    far = lax.ppermute(far, "tile", across)
    fetched = [lax.ppermute(piece, "dp", swap) for piece in cut]

    def both(pieces):
        return [half for piece in pieces for half in (piece, lax.ppermute(piece, "tile", mates))]

    (base,) = conv_call(video, None, [spatial_filter], depth, range(9), 16, light)
    *early, base = lax.optimization_barrier((*fetched[:-1], base))
    early = both(early)
    base, padded = conv_call(video, base, early, depth, range(middle), 16, light)
    other = lax.ppermute(fetched[-1], "tile", pairs)
    *late, base = lax.optimization_barrier((fetched[-1], other, base))
    late = both(late)
    c_y = lax.ppermute(c_y, "dp", swap)
    tail = c_y.reshape(-1, breadth, width)
    parts = [spatial_filter, *early, *late]
    *own, spatial = own_call(padded, base, biases[0], tail, parts, range(middle, 9), 16, blocks, light)
    temporal_parts = [temporal_filter, c_y]

    last = lax.ppermute(own[-1], "tile", across)
    mate = [lax.ppermute(block, "tile", mates) for block in own]
    out, temporal = mix_call(
        shape, far, own[:-1], mate[:-1], blocks[:-1], temporal_parts, [spatial], biases, None, 0, 12, tiles, heavy
    )
    (out,) = mix_call(
        shape, last, own[-1:], mate[-1:], blocks[-1:], [temporal], [], biases, out, sent - 1, blocks[-1], tiles, light
    )
    return out.reshape(videos.shape)


def padded_2(block, sides, width):
    for axis, dim in sides:
        count = lax.axis_size(axis)
        forward = [(i, i + 1) for i in range(count - 1)]
        backward = [(target, source) for source, target in forward]
        low = lax.ppermute(
            lax.slice_in_dim(block, block.shape[dim] - width, None, axis=dim), axis, forward
        )
        high = lax.ppermute(lax.slice_in_dim(block, 0, width, axis=dim), axis, backward)
        block = jnp.concatenate([low, block, high], axis=dim)
    return block


def spatial_term(padded, weight_piece):
    width = weight_piece.shape[1]
    height = padded.shape[2] - 2
    breadth = padded.shape[3] - 2
    columns = jnp.concatenate(
        [
            padded[:, :, row_off : row_off + height, col_off : col_off + breadth, :]
            for row_off in range(3)
            for col_off in range(3)
        ],
        axis=4,
    )
    matrix = weight_piece.reshape(9 * width, weight_piece.shape[2])
    return jnp.dot(columns.reshape(-1, 9 * width), matrix, preferred_element_type=jnp.float32)


def temporal_term(framed, weight_piece):
    width = weight_piece.shape[1]
    frames = framed.shape[1] - 2
    columns = jnp.concatenate([framed[:, lag : lag + frames] for lag in range(3)], axis=4)
    matrix = weight_piece.reshape(3 * width, weight_piece.shape[2])
    return jnp.dot(columns.reshape(-1, 3 * width), matrix, preferred_element_type=jnp.float32)


def any_device(videos, spatial_filter, temporal_filter, spatial_bias, temporal_bias):
    samples, frames, height, breadth, channels = videos.shape
    padded = jnp.pad(videos, ((0, 0), (0, 0), (1, 1), (1, 1), (0, 0)))
    summed = spatial_term(padded, lax.all_gather(spatial_filter, "dp", axis=1, tiled=True))
    activated = jax.nn.silu(summed + spatial_bias).astype(jnp.bfloat16)
    hidden = activated.reshape(samples, frames, height, breadth, channels)
    framed = padded_2(hidden, (("tile", 1),), 1)
    result = temporal_term(framed, lax.all_gather(temporal_filter, "dp", axis=1, tiled=True))
    return (result + temporal_bias).astype(jnp.bfloat16).reshape(videos.shape)


def per_device(videos, spatial_filter, *rest):
    near = (
        videos.shape[0] == 1
        and videos.shape[1] == 1
        and videos.shape[2] % 32 == 0
        and spatial_filter.shape[1] % (2 * videos.shape[3]) == 0
        and lax.axis_size("dp") == 2
        and lax.axis_size("tile") % 8 == 0
    )
    return (near_device if near else any_device)(videos, spatial_filter, *rest)


def solution(mesh):
    return jax.shard_map(
        per_device,
        mesh=mesh,
        in_specs=(
            P("dp", "tile", None, None, None),
            P(None, "dp", None),
            P(None, "dp", None),
            P(),
            P(),
        ),
        out_specs=P("dp", "tile", None, None, None),
        check_vma=False,
    )
```

```python
import functools

import jax
import jax.numpy as jnp
from jax import lax
from jax.experimental import pallas as pl
from jax.experimental.pallas import tpu as pltpu
from jax.sharding import PartitionSpec as P

ANY = pl.BlockSpec(memory_space=pltpu.HBM)


def dot(a, b):
    return jnp.dot(a, b, preferred_element_type=jnp.float32)


def silu(v):
    return v / (1 + jnp.exp(-v))


def halves(width):
    cut = width // 2
    return [slice(0, cut), slice(cut, width)]


def seat():
    return lax.axis_index("dp"), lax.rem(lax.axis_index("tile"), 2)


def half_starts(depth):
    _, core = seat()
    return [core * (depth // 2), (1 - core) * (depth // 2)]


def relay_starts(size):
    pair = lax.rem(lax.axis_index("tile") // 4, 2)
    return [pair * size, (1 - pair) * size]


def aligned(start):
    return pl.multiple_of(start, 16)


def rows_conv(padded, weights, taps, first, rows, breadth, columns):
    count = rows * breadth
    place = lax.rem(lax.broadcasted_iota(jnp.int32, (count, 1), 0), breadth)
    depth = padded.shape[2]
    lines = [padded[pl.ds(first + dy, rows)].reshape(count, depth) for dy in range(3)]

    def side(dx):
        mine = [(n, tap // 3) for n, tap in enumerate(taps) if tap % 3 == dx]
        matrix = jnp.concatenate([weights(n, columns) for n, _ in mine], axis=0)
        return dot(jnp.concatenate([lines[dy] for _, dy in mine], axis=1), matrix)

    total = side(1)
    total += jnp.where(place == 0, 0.0, pltpu.roll(side(0), 1, 0))
    total += jnp.where(place == breadth - 1, 0.0, pltpu.roll(side(2), count - 1, 0))
    return total


def cut_kernel(cuts, *refs):
    sources, targets, sem = refs[: len(cuts)], refs[len(cuts) : -1], refs[-1]
    copies = []
    for source, parts in zip(sources, cuts, strict=True):
        for where, _ in parts:
            n = len(copies)
            copies.append(pltpu.make_async_copy(source.at[where()], targets[n], sem.at[n]))
    for copy in copies:
        copy.start()
    for copy in copies:
        copy.wait()


def cut_call(sources, cuts, cost):
    shapes = [
        pltpu.VMEM(shape, source.dtype)
        for source, parts in zip(sources, cuts, strict=True)
        for _, shape in parts
    ]
    return pl.pallas_call(
        functools.partial(cut_kernel, cuts),
        in_specs=[ANY] * len(sources),
        out_specs=[pl.BlockSpec(memory_space=pltpu.VMEM)] * len(shapes),
        scratch_shapes=[pltpu.SemaphoreType.DMA((len(shapes),))],
        out_shape=shapes,
        cost_estimate=cost,
    )(*sources)


def block_spans(blocks, step, rows):
    spans = []
    for j, size in enumerate(blocks):
        at = sum(blocks[:j])
        low, high = max(at, step * rows), min(at + size, (step + 1) * rows)
        if high > low:
            spans.append((j, slice(low - at, high - at), slice(low - step * rows, high - step * rows)))
    return spans


def conv_kernel(rows, taps, held, video, *refs):
    refs = list(refs)
    base = None if held else refs.pop(0)
    weights, video_sem, part_sem = refs[-3:]
    out, padded = refs[-5:-3]
    parts = refs[:-5]
    height, breadth = video.shape[:2]
    steps = height // rows
    depth = padded.shape[2]
    pieces = 1 if held else 2
    i = pl.program_id(0)
    group, _ = seat()
    starts = [0] if held else half_starts(depth)

    def video_copy(j):
        channels = pl.ds(pl.multiple_of((group if held else 1 - group) * depth, 128), depth)
        return pltpu.make_async_copy(
            video.at[pl.ds(j * rows, rows), :, channels],
            padded.at[pl.ds(j * rows + 1, rows)],
            video_sem.at[j],
        )

    def part_copies():
        copies, begin = [], 0
        for n in range(0, len(parts), pieces):
            size = parts[n].shape[0]
            for p, start in enumerate(starts):
                there = weights.at[pl.ds(begin, size), pl.ds(aligned(start), parts[n + p].shape[1])]
                copies.append(pltpu.make_async_copy(parts[n + p], there, part_sem.at[n + p]))
            begin += size
        return copies

    @pl.when(i == 0)
    def _():
        video_copy(0).start()
        for copy in part_copies():
            copy.start()
        for j in range(1, steps):
            video_copy(j).start()
        padded[0] = jnp.zeros(padded.shape[1:], padded.dtype)
        padded[height + 1] = jnp.zeros(padded.shape[1:], padded.dtype)
        video_copy(0).wait()
        for copy in part_copies():
            copy.wait()

    @pl.when(i + 1 < steps)
    def _():
        video_copy(i + 1).wait()

    for columns in halves(out.shape[2]):
        total = rows_conv(padded, lambda n, c: weights[n, :, c], taps, i * rows, rows, breadth, columns)
        here = pl.ds(i * rows, rows)
        if not held:
            total += base[here, :, columns].reshape(total.shape)
        out[here, :, columns] = total.reshape(rows, breadth, -1)


IN_VMEM = pl.BlockSpec(memory_space=pltpu.VMEM)


def in_vmem(array):
    return pltpu.with_memory_space_constraint(array, pltpu.VMEM)


def conv_call(video, base, parts, depth, taps, rows, cost):
    height, breadth, _ = video.shape
    width = parts[0].shape[2]
    steps = height // rows
    held = base is None
    padded = (height + 2, breadth, depth)
    return pl.pallas_call(
        functools.partial(conv_kernel, rows, taps, held),
        grid=(steps,),
        in_specs=[ANY] + [IN_VMEM] * (not held) + [ANY] * len(parts),
        out_specs=[IN_VMEM] * (1 if held else 2),
        scratch_shapes=[pltpu.VMEM(padded, video.dtype)] * held
        + [
            pltpu.VMEM((len(taps), depth, width), video.dtype),
            pltpu.SemaphoreType.DMA((steps,)),
            pltpu.SemaphoreType.DMA((len(parts),)),
        ],
        out_shape=[pltpu.VMEM((height, breadth, width), jnp.float32)]
        + [pltpu.VMEM(padded, video.dtype)] * (not held),
        cost_estimate=cost,
        compiler_params=pltpu.CompilerParams(vmem_limit_bytes=24 * 2**20),
    )(video, *([] if held else [in_vmem(base)]), *parts)


def own_kernel(rows, blocks, taps, padded, base, bias, tail, *refs):
    parts = refs[: -len(blocks) - 2]
    outs, whole, part_sem = refs[-len(blocks) - 2 : -2], refs[-2], refs[-1]
    local, early, late = parts[0], parts[1:-4], parts[-4:]
    breadth, depth = padded.shape[1:]
    steps = (padded.shape[0] - 2) // rows
    group, _ = seat()
    other = (1 - group) * depth

    def early_copies():
        there = whole.at[:, pl.ds(aligned(group * depth), depth)]
        copies, begin = [pltpu.make_async_copy(local, there, part_sem.at[0])], 0
        for n in range(0, len(early), 2):
            size = early[n].shape[0]
            for p, start in enumerate(half_starts(depth)):
                there = whole.at[pl.ds(begin, size), pl.ds(aligned(other + start), early[n + p].shape[1])]
                copies.append(pltpu.make_async_copy(early[n + p], there, part_sem.at[1 + n + p]))
            begin += size
        return copies

    for copy in early_copies():
        copy.start()
    for n, first in enumerate(relay_starts(late[0].shape[0])):
        for p, start in enumerate(half_starts(depth)):
            part = late[2 * n + p]
            for tap in range(part.shape[0]):
                whole[taps[0] + first + tap, pl.ds(aligned(other + start), part.shape[1])] = part[tap]
    outs[-2][blocks[-2] :] = tail[...]

    def matrix(n, columns):
        return whole[taps[n], pl.ds(aligned(other), depth), columns]

    for step in range(steps):
        for columns in halves(whole.shape[2]):
            total = rows_conv(padded, matrix, taps, step * rows, rows, breadth, columns)
            total += base[step * rows : (step + 1) * rows, :, columns].reshape(total.shape)
            hidden = silu(total + bias[:, columns]).astype(padded.dtype).reshape(rows, breadth, -1)
            for j, there, here in block_spans(blocks, step, rows):
                outs[j][there, :, columns] = hidden[here]

    for copy in early_copies():
        copy.wait()


def own_call(padded, base, bias, tail, parts, taps, rows, blocks, cost):
    height, breadth, depth = padded.shape[0] - 2, *padded.shape[1:]
    width = base.shape[2]
    sizes = [*blocks[:-2], blocks[-2] + tail.shape[0], blocks[-1]]
    operands = [padded, base, bias, tail, *parts]
    near_too = [n for n in range(len(operands)) if n < 4 or n >= len(operands) - 4]
    for n in near_too:
        operands[n] = in_vmem(operands[n])
    return pl.pallas_call(
        functools.partial(own_kernel, rows, blocks, taps),
        in_specs=[IN_VMEM if n in near_too else ANY for n in range(len(operands))],
        out_specs=[IN_VMEM] * (len(blocks) + 1),
        scratch_shapes=[pltpu.SemaphoreType.DMA((len(parts) - 4,))],
        out_shape=[pltpu.VMEM((size, breadth, width), padded.dtype) for size in sizes]
        + [pltpu.VMEM((9, 2 * depth, width), padded.dtype)],
        cost_estimate=cost,
        compiler_params=pltpu.CompilerParams(vmem_limit_bytes=24 * 2**20),
    )(*operands)


def mix_kernel(rows, begin, sizes, given, tiles, *refs):
    refs = list(refs)

    def take(count):
        taken = refs[:count]
        del refs[:count]
        return taken

    blocks = len(sizes)
    owns, mates = take(blocks), take(blocks)
    (far_part,) = take(1)
    temporal_parts = take(1 if given else 2)
    spatial = take(0 if given else 1)
    spatial_bias, temporal_bias = take(2)
    take(1 if given else 0)
    (out,) = take(1)
    (temporal,) = temporal_parts if given else take(1)
    own, mate, far, far_sem = refs
    breadth, width = out.shape[1:]
    depth = temporal.shape[1]
    group, core = seat()
    tile = lax.axis_index("tile")
    present = jnp.where(core == 0, tile > 0, tile < tiles - 1)
    i = pl.program_id(0)

    if given:
        second = []
        (own,), (mate,), far = owns, mates, far_part
    else:
        second = [pltpu.make_async_copy(far_part, far.at[pl.ds(1, far_part.shape[0])], far_sem)]

    @pl.when(i == 0)
    def _():
        for copy in second:
            copy.start()
        if not given:
            far[0] = jnp.zeros(far.shape[1:], far.dtype)

    count = rows * breadth
    here = pl.ds(i * rows, rows)
    if not given:

        @pl.when(i == 0)
        def _():
            local, mine = temporal_parts
            held, part = depth // 2, depth // 4
            there = (1 - group) * held
            temporal[:, pl.ds(aligned(group * held), held)] = local[...]
            temporal[:, pl.ds(aligned(there + core * part), part)] = mine[...]
            tail = mates[-1][sizes[-1] :].reshape(3, part, width)
            temporal[:, pl.ds(aligned(there + (1 - core) * part), part)] = tail

        for step in range(sum(sizes) // rows):

            @pl.when(i == step)
            def _():
                for j, there, here in block_spans(sizes, step, rows):
                    own[here], mate[here] = owns[j][there], mates[j][there]

        own_lines, mate_lines = (ref[...].reshape(count, depth) for ref in (own, mate))
    else:
        own_lines, mate_lines = (ref[here].reshape(count, depth) for ref in (own, mate))
    mate_tap, far_tap = 2 - 2 * core, 2 * core

    def matrix(tap, columns):
        return temporal[tap, :, columns]

    def spatial_rows(tap, columns):
        return spatial[0][tap, :, columns]

    def product(lines, taps, columns):
        return dot(jnp.concatenate(lines, axis=1), jnp.concatenate([matrix(tap, columns) for tap in taps], axis=0))

    def masked(lines):
        return jnp.where(present, lines, jnp.zeros_like(lines))

    def put(total, columns):
        total += temporal_bias[:, columns]
        out[:, :, columns] = total.astype(out.dtype).reshape(rows, breadth, -1)

    if given:
        lines = [own_lines, mate_lines, masked(far[here].reshape(count, depth))]
        for columns in halves(width):
            put(product(lines, (1, mate_tap, far_tap), columns), columns)
        return

    totals = [product([own_lines, mate_lines], (1, mate_tap), columns) for columns in halves(width)]

    @pl.when(i == 0)
    def _():
        for copy in second:
            copy.wait()

    far_lines = jnp.concatenate(
        [
            silu(
                rows_conv(far, spatial_rows, range(9), i * rows, rows, breadth, columns) + spatial_bias[:, columns]
            ).astype(far.dtype)
            for columns in halves(depth)
        ],
        axis=1,
    )
    far_lines = masked(far_lines)
    for total, columns in zip(totals, halves(width), strict=True):
        put(total + dot(far_lines, matrix(far_tap, columns)), columns)


def mix_call(shape, far, owns, mates, sizes, temporal_parts, spatial, biases, before, begin, rows, tiles, cost):
    height, breadth, width = shape
    dtype = far.dtype
    count, depth = sum(sizes), far.shape[2]
    given = before is not None
    operands = [*owns, *mates, far, *temporal_parts, *spatial]
    specs = [ANY] * len(operands)
    for n in range(len(operands)):
        if given or n != 2 * len(owns):
            specs[n] = IN_VMEM
            operands[n] = in_vmem(operands[n])
    out_shape = [jax.ShapeDtypeStruct(shape, dtype)]
    out_specs = [pl.BlockSpec((rows, breadth, width), lambda i: (i + begin // rows, 0, 0))]
    if not given:
        out_shape.append(pltpu.VMEM((3, depth, width), dtype))
        out_specs.append(IN_VMEM)
    return pl.pallas_call(
        functools.partial(mix_kernel, rows, begin, sizes, given, tiles),
        grid=(count // rows,),
        in_specs=specs + [IN_VMEM, IN_VMEM] + [ANY] * given,
        out_specs=out_specs,
        scratch_shapes=[
            pltpu.VMEM((16, 128) if given else (rows, breadth, depth), dtype),
            pltpu.VMEM((16, 128) if given else (rows, breadth, depth), dtype),
            pltpu.VMEM((16, 128) if given else (count + 2, breadth, depth), dtype),
            pltpu.SemaphoreType.DMA,
        ],
        out_shape=out_shape,
        input_output_aliases={len(operands) + 2: 0} if given else {},
        cost_estimate=cost,
        compiler_params=pltpu.CompilerParams(vmem_limit_bytes=40 * 2**20),
    )(*operands, *map(in_vmem, biases), *([before] if given else []))


def near_device(videos, spatial_filter, temporal_filter, spatial_bias, temporal_bias):
    shape = videos.shape[2:]
    height, breadth, channels = shape
    video = videos.reshape(shape)
    biases = [spatial_bias.reshape(1, -1), temporal_bias.reshape(1, -1)]
    tiles = lax.axis_size("tile")
    depth, width = spatial_filter.shape[1:]
    half = depth // 2
    swap = [(0, 1), (1, 0)]
    mates = [(i, i ^ 1) for i in range(tiles)]
    pairs = [(i, i ^ 4) for i in range(tiles)]
    across = [pair for i in range(1, tiles - 1, 2) for pair in ((i, i + 1), (i + 1, i))]
    light = pl.CostEstimate(flops=1000, bytes_accessed=1000, transcendentals=0)
    heavy = pl.CostEstimate(flops=10**12, bytes_accessed=1000, transcendentals=0)

    def mine(first, count):
        return lambda: (pl.ds(first, count), pl.ds(aligned(half_starts(depth)[0]), half))

    def relayed():
        return mine(middle + relay_starts(relay)[0], relay)()

    unit = height // 32
    blocks = tuple(unit * block for block in (9, 9, 6, 8))
    sent = height - blocks[-1] + 1
    taps = [(0, 3), (3, 2)]
    middle, relay = 5, 2
    cuts = [
        [(mine(first, count), (count, half, width)) for first, count in taps] + [(relayed, (relay, half, width))],
        [(mine(0, 3), (3, half, width))],
        [(lambda: (pl.ds(0, sent),), (sent, breadth, channels))],
    ]
    *cut, c_y, far = cut_call([spatial_filter, temporal_filter, video], cuts, light)
    far = lax.ppermute(far, "tile", across)
    fetched = [lax.ppermute(piece, "dp", swap) for piece in cut]

    def both(pieces):
        return [half for piece in pieces for half in (piece, lax.ppermute(piece, "tile", mates))]

    (base,) = conv_call(video, None, [spatial_filter], depth, range(9), 16, light)
    *early, base = lax.optimization_barrier((*fetched[:-1], base))
    early = both(early)
    base, padded = conv_call(video, base, early, depth, range(middle), 16, light)
    other = lax.ppermute(fetched[-1], "tile", pairs)
    *late, base = lax.optimization_barrier((fetched[-1], other, base))
    late = both(late)
    c_y = lax.ppermute(c_y, "dp", swap)
    tail = c_y.reshape(-1, breadth, width)
    parts = [spatial_filter, *early, *late]
    *own, spatial = own_call(padded, base, biases[0], tail, parts, range(middle, 9), 8, blocks, light)
    temporal_parts = [temporal_filter, c_y]

    last = lax.ppermute(own[-1], "tile", across)
    mate = [lax.ppermute(block, "tile", mates) for block in own]
    out, temporal = mix_call(
        shape, far, own[:-1], mate[:-1], blocks[:-1], temporal_parts, [spatial], biases, None, 0, 12, tiles, heavy
    )
    (out,) = mix_call(
        shape, last, own[-1:], mate[-1:], blocks[-1:], [temporal], [], biases, out, sent - 1, blocks[-1], tiles, light
    )
    return out.reshape(videos.shape)


def padded_2(block, sides, width):
    for axis, dim in sides:
        count = lax.axis_size(axis)
        forward = [(i, i + 1) for i in range(count - 1)]
        backward = [(target, source) for source, target in forward]
        low = lax.ppermute(
            lax.slice_in_dim(block, block.shape[dim] - width, None, axis=dim), axis, forward
        )
        high = lax.ppermute(lax.slice_in_dim(block, 0, width, axis=dim), axis, backward)
        block = jnp.concatenate([low, block, high], axis=dim)
    return block


def spatial_term(padded, weight_piece):
    width = weight_piece.shape[1]
    height = padded.shape[2] - 2
    breadth = padded.shape[3] - 2
    columns = jnp.concatenate(
        [
            padded[:, :, row_off : row_off + height, col_off : col_off + breadth, :]
            for row_off in range(3)
            for col_off in range(3)
        ],
        axis=4,
    )
    matrix = weight_piece.reshape(9 * width, weight_piece.shape[2])
    return jnp.dot(columns.reshape(-1, 9 * width), matrix, preferred_element_type=jnp.float32)


def temporal_term(framed, weight_piece):
    width = weight_piece.shape[1]
    frames = framed.shape[1] - 2
    columns = jnp.concatenate([framed[:, lag : lag + frames] for lag in range(3)], axis=4)
    matrix = weight_piece.reshape(3 * width, weight_piece.shape[2])
    return jnp.dot(columns.reshape(-1, 3 * width), matrix, preferred_element_type=jnp.float32)


def any_device(videos, spatial_filter, temporal_filter, spatial_bias, temporal_bias):
    samples, frames, height, breadth, channels = videos.shape
    padded = jnp.pad(videos, ((0, 0), (0, 0), (1, 1), (1, 1), (0, 0)))
    summed = spatial_term(padded, lax.all_gather(spatial_filter, "dp", axis=1, tiled=True))
    activated = jax.nn.silu(summed + spatial_bias).astype(jnp.bfloat16)
    hidden = activated.reshape(samples, frames, height, breadth, channels)
    framed = padded_2(hidden, (("tile", 1),), 1)
    result = temporal_term(framed, lax.all_gather(temporal_filter, "dp", axis=1, tiled=True))
    return (result + temporal_bias).astype(jnp.bfloat16).reshape(videos.shape)


def per_device(videos, spatial_filter, *rest):
    near = (
        videos.shape[0] == 1
        and videos.shape[1] == 1
        and videos.shape[2] % 32 == 0
        and spatial_filter.shape[1] % (2 * videos.shape[3]) == 0
        and lax.axis_size("dp") == 2
        and lax.axis_size("tile") % 8 == 0
    )
    return (near_device if near else any_device)(videos, spatial_filter, *rest)


def solution(mesh):
    return jax.shard_map(
        per_device,
        mesh=mesh,
        in_specs=(
            P("dp", "tile", None, None, None),
            P(None, "dp", None),
            P(None, "dp", None),
            P(),
            P(),
        ),
        out_specs=P("dp", "tile", None, None, None),
        check_vma=False,
    )
```
